256 devices in a mesh: dp: 32 (over z_lo, x, core), blk: 8 (over y, z_hi).
Axes of the slice: x: 4, y: 4, z: 8 (z_hi: 2, z_lo: 4; z = z_hi * 4 + z_lo), core: 2. Of those that a mesh axis runs over, the one named last changes fastest.
Arguments:
- tokens: bfloat16 [4096, 8192], P('dp', 'blk'), may hold values from -6 to 6
- gate_right: bfloat16 [256, 32, 448], P(None, 'blk'), may hold values from -0.375 to 0.375
- gate_left: bfloat16 [448, 32, 448], P(None, 'blk'), may hold values from -0.25 to 0.25
- upward_right: bfloat16 [256, 32, 448], P(None, 'blk'), may hold values from -0.375 to 0.375
- upward_left: bfloat16 [448, 32, 448], P(None, 'blk'), may hold values from -0.25 to 0.25
- down_right: bfloat16 [448, 32, 256], P(None, 'blk'), may hold values from -0.25 to 0.25
- down_left: bfloat16 [256, 32, 256], P(None, 'blk'), may hold values from -0.375 to 0.375
- cotangent: bfloat16 [4096, 8192], P('dp', 'blk'), may hold values from -6 to 6
Outputs:
- mixed: bfloat16 [4096, 8192], P('dp', 'blk')
- grad_tokens: bfloat16 [4096, 8192], P('dp', 'blk')
- gate_right_grad: float32 [256, 32, 448], P('dp', 'blk')
- gate_left_grad: float32 [448, 32, 448], P('dp', 'blk')
- upward_right_grad: float32 [256, 32, 448], P('dp', 'blk')
- upward_left_grad: float32 [448, 32, 448], P('dp', 'blk')
- down_right_grad: float32 [448, 32, 256], P('dp', 'blk')
- down_left_grad: float32 [256, 32, 256], P('dp', 'blk')
The draws below stay inside these ranges and needn't reach their ends.
All inputs are finite; a program needn't handle non-finite values.
Results may differ from the reference program's by a relative error of at most 0.0072.
Values may be sent and summed in bfloat16 or wider, within the bound.
A program may use at most 128 MiB of HBM per device.

```python
import jax
import jax.numpy as jnp

D = 8192
NB = 32
DB = 256
MB = 448
MS = 14
CS = 8
TOKENS = 4096


def levels(stream_key, shape, pieces, least, largest):
    loudness = 1.0
    for position, shards_of in pieces:
        heights = jax.random.uniform(jax.random.fold_in(jax.random.fold_in(stream_key, 6), position), (shards_of,), jnp.float32, least / len(pieces), largest / len(pieces))
        loudness = loudness * jnp.repeat(jnp.exp(heights), shape[position] // shards_of).reshape((-1,) + (1,) * (len(shape) - 1 - position))
    return loudness


def normal_values(own_key, extent, deviation, limit, pieces=(), kind=jnp.bfloat16):
    level = levels(own_key, extent, pieces, -0.22, 0.18) if pieces else 1.0
    entries = jax.random.normal(own_key, extent, jnp.float32) * deviation * level
    return jnp.minimum(jnp.maximum(entries, -limit), limit).astype(kind)


def setup_inputs(seed: int = 0) -> dict:
    key_of = jax.random.split(jax.random.key(seed), 9)
    tokens = normal_values(key_of[0], (TOKENS, D), 1.0, 6.0, ((0, 32), (1, 8)))
    gate_right = normal_values(key_of[1], (DB, NB, MB), DB ** -0.5, 0.375, ((1, 8),))
    gate_left = normal_values(key_of[2], (MB, NB, MB), MB ** -0.5, 0.25, ((1, 8),))
    upward_right = normal_values(key_of[3], (DB, NB, MB), DB ** -0.5, 0.375, ((1, 8),))
    upward_left = normal_values(key_of[4], (MB, NB, MB), MB ** -0.5, 0.25, ((1, 8),))
    down_right = normal_values(key_of[5], (MB, NB, DB), MB ** -0.5, 0.25, ((1, 8),))
    down_left = normal_values(key_of[6], (DB, NB, DB), DB ** -0.5, 0.375, ((1, 8),))
    cotangent = normal_values(key_of[7], (TOKENS, D), 1.0, 6.0, ((0, 32), (1, 8)))
    return {"tokens": tokens, "gate_right": gate_right, "gate_left": gate_left, "upward_right": upward_right, "upward_left": upward_left, "down_right": down_right, "down_left": down_left, "cotangent": cotangent}


def right_mix(source, weight, width_out):
    four = weight.reshape(weight.shape[0], NB, NB, width_out // NB).astype(jnp.float32)
    mixed_four = jnp.einsum("tkb,bkjr->jkrt", source, four)
    return mixed_four.astype(jnp.bfloat16).reshape(NB, -1, source.shape[0])


def left_mix(seen, weight):
    return jnp.einsum("jmt,mjn->jnt", seen.astype(jnp.float32), weight.astype(jnp.float32))


def back_left(gradient, weight):
    flow = jnp.einsum("jnt,mjn->jmt", gradient.astype(jnp.float32), weight.astype(jnp.float32))
    return flow.astype(jnp.bfloat16).reshape(NB, NB, -1, gradient.shape[2])


def reference(tokens, gate_right, gate_left, upward_right, upward_left, down_right, down_left, cotangent):
    grad_scale = TOKENS ** -0.5
    inputs = tokens.astype(jnp.float32).reshape(TOKENS, NB, DB)
    gate_seen = right_mix(inputs, gate_right, MB)
    upward_seen = right_mix(inputs, upward_right, MB)
    gate_pre = left_mix(gate_seen, gate_left)
    upward_pre = left_mix(upward_seen, upward_left)
    gate_sigmoid = jax.nn.sigmoid(gate_pre)
    activated = gate_pre * gate_sigmoid
    hidden = (activated * upward_pre).astype(jnp.bfloat16)
    hidden_wide = hidden.astype(jnp.float32)
    down_seen = jnp.einsum("knt,nkjs->jkst", hidden_wide, down_right.reshape(MB, NB, NB, CS).astype(jnp.float32))
    down_seen = down_seen.astype(jnp.bfloat16).reshape(NB, DB, TOKENS)
    down_out = left_mix(down_seen, down_left)
    mixed = jnp.transpose(down_out, (2, 0, 1)).reshape(TOKENS, D).astype(jnp.bfloat16)
    upstream = cotangent.astype(jnp.float32).reshape(TOKENS, NB, DB)
    down_flow = jnp.einsum("tjn,mjn->jmt", upstream, down_left.astype(jnp.float32))
    down_back = down_flow.astype(jnp.bfloat16).reshape(NB, NB, CS, TOKENS).astype(jnp.float32)
    down_four = down_right.reshape(MB, NB, NB, CS).astype(jnp.float32)
    hidden_flow = jnp.einsum("jkst,nkjs->knt", down_back, down_four)
    gate_grad = (hidden_flow * upward_pre * gate_sigmoid * (1.0 + gate_pre * (1.0 - gate_sigmoid))).astype(jnp.bfloat16)
    upward_grad = (hidden_flow * activated).astype(jnp.bfloat16)
    gate_back = back_left(gate_grad, gate_left).astype(jnp.float32)
    upward_back = back_left(upward_grad, upward_left).astype(jnp.float32)
    gate_four = gate_right.reshape(DB, NB, NB, MS).astype(jnp.float32)
    upward_four = upward_right.reshape(DB, NB, NB, MS).astype(jnp.float32)
    token_flow = jnp.einsum("jkrt,bkjr->tkb", gate_back, gate_four) + jnp.einsum("jkrt,bkjr->tkb", upward_back, upward_four)
    grad_tokens = token_flow.reshape(TOKENS, D).astype(jnp.bfloat16)
    down_left_grad = grad_scale * jnp.einsum("jmt,tjn->mjn", down_seen.astype(jnp.float32), upstream)
    down_right_grad = grad_scale * jnp.einsum("knt,jkst->nkjs", hidden_wide, down_back).reshape(MB, NB, DB)
    gate_left_grad = grad_scale * jnp.einsum("jmt,jnt->mjn", gate_seen.astype(jnp.float32), gate_grad.astype(jnp.float32))
    upward_left_grad = grad_scale * jnp.einsum("jmt,jnt->mjn", upward_seen.astype(jnp.float32), upward_grad.astype(jnp.float32))
    gate_right_grad = grad_scale * jnp.einsum("tkb,jkrt->bkjr", inputs, gate_back).reshape(DB, NB, MB)
    upward_right_grad = grad_scale * jnp.einsum("tkb,jkrt->bkjr", inputs, upward_back).reshape(DB, NB, MB)
    return (mixed, grad_tokens, gate_right_grad, gate_left_grad, upward_right_grad, upward_left_grad, down_right_grad, down_left_grad)
```

```python
import types

import jax
import jax.numpy as jnp
import numpy as np
from jax import lax
from jax.experimental import pallas as pl
from jax.experimental.pallas import tpu as pltpu
from jax.sharding import PartitionSpec as P

BF = jnp.bfloat16
F32 = jnp.float32
MESH = pl.DeviceIdType.MESH

NB = 32
KB = 4
DB = 256
MB = 448
MS = 14
T = 128
X, Z, Y = 4, 4, 4
OFFS = ((0, 1), (1, 1), (3, 1), (2, 1), (1, 0), (3, 0), (2, 0))


def permutations():
    pair = np.zeros((448, 448), np.float32)
    for b in range(4):
        for zh in range(2):
            for a in range(4):
                for r in range(MS):
                    pair[((b * 2 + zh) * 4 + a) * MS + r, ((zh * 4 + a) * 4 + b) * MS + r] = 1.0
    spread = np.zeros((2, 256, 448), np.float32)
    twin = np.zeros((2, 2, 256, 256), np.float32)
    for c in range(2):
        for x in range(X):
            for z in range(Z):
                d = z * 8 + x * 2 + c
                for i in range(MS):
                    spread[c, (x * 4 + z) * 16 + i, d * MS + i] = 1.0
                for q in range(2):
                    for i in range(8):
                        twin[q, c, (x * 4 + z) * 16 + q * 8 + i, d * 8 + i] = 1.0
    return (
        np.asarray(pair, jnp.bfloat16),
        np.asarray(spread.reshape(512, 448), jnp.bfloat16),
        np.asarray(twin.reshape(2, 512, 256), jnp.bfloat16),
    )


def nn(a, b):
    return lax.dot_general(a, b, (((1,), (0,)), ((), ())), preferred_element_type=F32)


def nt(a, b):
    return lax.dot_general(a, b, (((1,), (1,)), ((), ())), preferred_element_type=F32)


def tn(a, b):
    return lax.dot_general(a, b, (((0,), (0,)), ((), ())), preferred_element_type=F32)


INPUTS = ("x", "g", "wgr", "wur", "wdl", "pair", "wgl", "wul", "wdr", "spread", "twin")
SHAPES = {
    "x": (T, KB * DB),
    "g": (T, KB * DB),
    "wgr": (KB, MB, DB),
    "wur": (KB, MB, DB),
    "wdl": (KB, DB, DB),
    "pair": (448, 448),
    "wgl": (KB, MB, MB),
    "wul": (KB, MB, MB),
    "wdr": (KB, DB, MB),
    "spread": (512, 448),
    "twin": (2, 512, 256),
}
GROUPS = (("left", 4, 896), ("dright", 4, 256), ("dleft", 2, 256), ("gright", 1, 896), ("uright", 1, 896))
OUTS = ("mixed", "gtok") + tuple("o_" + name for name, _, _ in GROUPS)


def scratch_list():
    out = []

    def add(name, shape, dtype=BF):
        out.append((name, pltpu.VMEM(shape, dtype)))

    for name in INPUTS:
        add("v_" + name, SHAPES[name])
    out.append(("in_sem", pltpu.SemaphoreType.DMA((len(INPUTS),))))
    for name, rows in (("ag", 224), ("au", 224), ("dg", 224), ("du", 224), ("b", 128), ("c", 128)):
        add("s_" + name, (8, rows, T))
        add("r_" + name, (8, rows, T))
        out.append(("ss_" + name, pltpu.SemaphoreType.DMA((7,))))
        out.append(("rs_" + name, pltpu.SemaphoreType.DMA((7,))))
    add("flow", (KB, MB, T), F32)
    for name in ("seen_g", "seen_u", "back_g", "back_u"):
        add(name, (KB, Y, 112, T))
    add("gate_pre", (KB, T, MB), F32)
    add("act", (KB, T, MB), F32)
    add("slope", (KB, T, MB), F32)
    add("hidden", (KB, T, MB))
    add("grad_g", (KB, T, MB))
    add("grad_u", (KB, T, MB))
    add("dback32", (KB, 8, 4, 8, T), F32)
    add("dseen32", (KB, 8, 4, 8, T), F32)
    add("dback", (KB, DB, T))
    add("dseen", (KB, DB, T))
    add("lhs_left", (KB, 2, 256, 256))
    add("rhs_left", (KB, 256, 896))
    add("lhs_dright", (KB, 2, 256, T))
    add("lhs_dleft", (2, 2, 256, 256))
    add("lhs_right", (2, 256, 512))
    add("rhs_gright", (896, 512))
    add("rhs_uright", (896, 512))
    for name, count, lanes in GROUPS:
        add("s0_" + name, (count, 256, lanes))
        add("r0_" + name, (count, 256, lanes))
        add("s1_" + name, (count, X, 64, lanes))
        add("r1_" + name, (count, 3, 64, lanes))
        add("s2_" + name, (count, Z, 16, lanes))
        add("r2_" + name, (3, count, 16, lanes))
        for kind in ("ss0_", "rs0_"):
            out.append((kind + name, pltpu.SemaphoreType.DMA((count,))))
        for kind in ("ss1_", "rs1_"):
            out.append((kind + name, pltpu.SemaphoreType.DMA((count * 3,))))
        for kind in ("ss2_", "rs2_"):
            out.append((kind + name, pltpu.SemaphoreType.DMA((3,))))
    return out


def loop(count, body):
    lax.fori_loop(0, count, lambda i, _: (body(i), 0)[1], 0)


def kernel(scale, names, *refs):
    r = types.SimpleNamespace(**dict(zip(names, refs)))
    v = vars(r)
    dp = lax.axis_index("dp")
    blk = lax.axis_index("blk")
    core, x, z = dp % 2, (dp // 2) % X, dp // 8
    y, zh = blk // 2, blk % 2
    pending = []

    loads = {}
    for i, name in enumerate(INPUTS):
        loads[name] = pltpu.make_async_copy(v["h_" + name], v["v_" + name], r.in_sem.at[i])
        loads[name].start()

    def need(*which):
        for name in which:
            loads[name].wait()

    def blk_peer(dy, dz):
        return ((y + dy) % Y) * 2 + (zh + dz) % 2

    def dp_id(z_, x_, c_):
        return (z_ * 8 + x_ * 2 + c_, blk)

    core_id = dp_id(z, x, 1 - core)
    x_ids = [dp_id(z, (x + d) % X, core) for d in (1, 2, 3)]
    z_ids = [dp_id((z + d) % Z, x, core) for d in (1, 2, 3)]
    everyone = [(dp, blk_peer(dy, dz)) for dy, dz in OFFS] + [core_id] + x_ids + z_ids

    barrier = pltpu.get_barrier_semaphore()
    for who in everyone:
        pl.semaphore_signal(barrier, inc=1, device_id=who, device_id_type=MESH)

    def remote(src, dst, ss, rs, who):
        copy = pltpu.make_async_remote_copy(
            src_ref=src, dst_ref=dst, send_sem=ss, recv_sem=rs, device_id=who, device_id_type=MESH
        )
        copy.start()
        pending.append(copy)
        return copy

    def exchange(name):
        s, d, ss, rs = (v[k + name] for k in ("s_", "r_", "ss_", "rs_"))
        out = {}
        for i, (dy, dz) in enumerate(OFFS):
            p = blk_peer(dy, dz)
            out[dy, dz] = remote(s.at[p], d.at[blk], ss.at[i], rs.at[i], (dp, p))
        d[blk] = s[blk]
        return out

    def slabs(name):
        for p in range(8):
            rows = r.flow[:, p * 56 : (p + 1) * 56, :]
            v["s_" + name][p] = rows.reshape(224, T).astype(BF)

    def unslab(name, copies, out):
        for dy in range(4):
            for dz in range(2):
                if (dy, dz) != (0, 0):
                    copies[dy, dz].wait_recv()
            ys = (y - dy + Y) % Y
            two = v["r_" + name][pl.ds(ys * 2, 2)].reshape(448, T)
            moved = nn(r.v_pair[...], two).astype(BF)
            out[:, pl.ds(ys, 1)] = moved.reshape(KB, 1, 112, T)

    def unswap(name, copies, wide, out):
        for copy in copies.values():
            copy.wait_recv()

        def one(s):
            got = v["r_" + name][s].astype(F32).reshape(4, 4, 8, T)
            for a in range(4):
                for b in range(4):
                    wide[b, s, a] = got[a, b]

        loop(8, one)

        def two(b):
            out[b] = wide[b].reshape(DB, T).astype(BF)

        loop(KB, two)

    def right(weight):
        for k in range(KB):
            r.flow[k] = nt(weight[k], r.v_x[:, k * DB : (k + 1) * DB])

    need("x", "wgr")
    right(r.v_wgr)
    slabs("ag")
    pl.semaphore_wait(barrier, len(everyone))
    from_ag = exchange("ag")
    need("wur")
    right(r.v_wur)
    slabs("au")
    from_au = exchange("au")

    need("g", "wdl")
    for j in range(KB):
        f = nt(r.v_wdl[j], r.v_g[:, j * DB : (j + 1) * DB]).astype(BF)
        r.s_c[:, j * 32 : (j + 1) * 32, :] = f.reshape(8, 32, T)
    from_c = exchange("c")

    need("pair", "spread", "twin")
    r.rhs_gright[...] = jnp.zeros_like(r.rhs_gright)
    r.rhs_uright[...] = jnp.zeros_like(r.rhs_uright)
    for k in range(KB):
        f = nt(r.v_twin[k // 2], r.v_x[:, k * DB : (k + 1) * DB]).astype(BF)
        r.lhs_right[:, :, k * T : (k + 1) * T] = f.reshape(2, 256, T)
    need("wgl", "wul", "wdr")

    unslab("ag", from_ag, r.seen_g)

    def gate(j):
        r.gate_pre[j] = tn(r.seen_g[j].reshape(MB, T), r.v_wgl[j])

    loop(KB, gate)

    unslab("au", from_au, r.seen_u)

    def forward(j):
        up = tn(r.seen_u[j].reshape(MB, T), r.v_wul[j])
        pre = r.gate_pre[j]
        sig = jax.nn.sigmoid(pre)
        act = pre * sig
        hidden = (act * up).astype(BF)
        r.act[j] = act
        r.slope[j] = up * sig * (1.0 + pre * (1.0 - sig))
        r.hidden[j] = hidden
        f = nt(r.v_wdr[j], hidden).astype(BF)
        r.s_b[:, pl.ds(pl.multiple_of(j * 32, 32), 32), :] = f.reshape(8, 32, T)

    loop(KB, forward)
    from_b = exchange("b")

    unswap("c", from_c, r.dback32, r.dback)

    def backward(j):
        hf = tn(r.dback[j], r.v_wdr[j])
        gg = (hf * r.slope[j]).astype(BF)
        ug32 = hf * r.act[j]
        ug = ug32.astype(BF)
        r.grad_g[j] = gg
        r.grad_u[j] = ug
        r.flow[j] = nt(r.v_wgl[j], gg)

    loop(KB, backward)
    slabs("dg")
    from_dg = exchange("dg")

    def backward_up(j):
        r.flow[j] = nt(r.v_wul[j], r.grad_u[j])

    loop(KB, backward_up)
    slabs("du")
    from_du = exchange("du")

    moves = {}

    def start_core(name, count, half):
        s0, r0, ss, rs = (v[k + name] for k in ("s0_", "r0_", "ss0_", "rs0_"))
        for j in range(count):
            s0[j] = half(j, 1 - core).astype(BF)
            moves[name, 0, j] = remote(s0.at[j], r0.at[j], ss.at[j], rs.at[j], core_id)

    def start_x(name, count, half):
        r0, s1, r1, ss, rs = (v[k + name] for k in ("r0_", "s1_", "r1_", "ss1_", "rs1_"))
        for j in range(count):
            own = half(j, core)
            moves[name, 0, j].wait_recv()
            s1[j] = (own + r0[j].astype(F32)).astype(BF).reshape(s1.shape[1:])
            for i in (0, 2, 1):
                moves[name, 1, j, i] = remote(
                    s1.at[j, (x + i + 1) % X],
                    r1.at[j, i],
                    ss.at[j * 3 + i],
                    rs.at[j * 3 + i],
                    x_ids[i],
                )

    def start_z(name, count):
        s1, r1, s2, r2, ss, rs = (
            v[k + name] for k in ("s1_", "r1_", "s2_", "r2_", "ss2_", "rs2_")
        )
        for j in range(count):
            for i in range(3):
                moves[name, 1, j, i].wait_recv()
            total = s1[j, x].astype(F32)
            for i in range(3):
                total = total + r1[j, i].astype(F32)
            s2[j] = total.astype(BF).reshape(s2.shape[1:])
        for i in range(3):
            moves[name, 2, i] = remote(
                s2.at[:, (z + i + 1) % Z], r2.at[i], ss.at[i], rs.at[i], z_ids[i]
            )

    def finish(name, count):
        s2, r2, out = v["s2_" + name], v["r2_" + name], v["o_" + name]
        for i in range(3):
            moves[name, 2, i].wait_recv()
        for j in range(count):
            total = s2[j, z].astype(F32)
            for i in range(3):
                total = total + r2[i, j].astype(F32)
            out[j] = scale * total

    def sides(j):
        f = nn(r.v_spread[...], r.seen_g[j].reshape(MB, T)).astype(BF)
        r.lhs_left[j, :, :, :T] = f.reshape(2, 256, T)
        f = nn(r.v_spread[...], r.seen_u[j].reshape(MB, T)).astype(BF)
        r.lhs_left[j, :, :, T:] = f.reshape(2, 256, T)
        f = nt(r.v_spread[...], r.hidden[j]).astype(BF)
        r.lhs_dright[j] = f.reshape(2, 256, T)
        gate_part = jnp.concatenate([r.grad_g[j], jnp.zeros((T, 448), BF)], axis=1)
        up_part = jnp.concatenate([jnp.zeros((T, 448), BF), r.grad_u[j]], axis=1)
        r.rhs_left[j, :T, :] = gate_part
        r.rhs_left[j, T:, :] = up_part

    loop(KB, sides)

    def left_half(j, c):
        return nn(r.lhs_left[j, c], r.rhs_left[j])

    def dright_half(j, c):
        return nt(r.lhs_dright[j, c], r.dback[j])

    def dleft_half(q, c):
        rows = [r.v_g[:, (2 * q + i) * DB : (2 * q + i + 1) * DB] for i in range(2)]
        return nn(r.lhs_dleft[q, c], jnp.concatenate(rows, axis=0))

    start_core("left", 4, left_half)
    start_core("dright", 4, dright_half)
    start_x("left", 4, left_half)
    start_x("dright", 4, dright_half)

    unswap("b", from_b, r.dseen32, r.dseen)
    for j in range(KB):
        r.mixed[:, j * DB : (j + 1) * DB] = tn(r.dseen[j], r.v_wdl[j]).astype(BF)
        f = nn(r.v_twin[j % 2], r.dseen[j]).astype(BF)
        r.lhs_dleft[j // 2, :, :, (j % 2) * T : (j % 2 + 1) * T] = f.reshape(2, 256, T)
    start_core("dleft", 2, dleft_half)
    start_x("dleft", 2, dleft_half)

    def spread_back(back, rhs):
        for k in range(KB):
            q, i = k // 2, k % 2
            rhs[i * MB : (i + 1) * MB, k * T : (k + 1) * T] = back[k].reshape(MB, T)

    def gright_half(j, c):
        return nt(r.lhs_right[c], r.rhs_gright[...])

    def uright_half(j, c):
        return nt(r.lhs_right[c], r.rhs_uright[...])

    unslab("dg", from_dg, r.back_g)
    spread_back(r.back_g, r.rhs_gright)
    start_core("gright", 1, gright_half)
    start_x("gright", 1, gright_half)
    start_z("left", 4)
    start_z("dright", 4)
    start_z("dleft", 2)

    unslab("du", from_du, r.back_u)
    spread_back(r.back_u, r.rhs_uright)
    start_core("uright", 1, uright_half)
    start_x("uright", 1, uright_half)

    for k in range(KB):
        total = tn(r.back_g[k].reshape(MB, T), r.v_wgr[k])
        total = total + tn(r.back_u[k].reshape(MB, T), r.v_wur[k])
        r.gtok[:, k * DB : (k + 1) * DB] = total.astype(BF)

    start_z("gright", 1)
    finish("left", 4)
    finish("dright", 4)
    finish("dleft", 2)
    start_z("uright", 1)
    finish("gright", 1)
    finish("uright", 1)
    for copy in pending:
        copy.wait_send()


def local(tokens, gate_right, gate_left, upward_right, upward_left, down_right, down_left, cotangent):
    scale = float(tokens.shape[0] * lax.axis_size("dp")) ** (-0.5)
    pair, spread, twin = permutations()
    given = {
        "x": tokens,
        "g": cotangent,
        "wgr": jnp.transpose(gate_right, (1, 2, 0)),
        "wur": jnp.transpose(upward_right, (1, 2, 0)),
        "wdl": jnp.transpose(down_left, (1, 0, 2)),
        "pair": jnp.asarray(pair),
        "wgl": jnp.transpose(gate_left, (1, 0, 2)),
        "wul": jnp.transpose(upward_left, (1, 0, 2)),
        "wdr": jnp.transpose(down_right, (1, 2, 0)),
        "spread": jnp.asarray(spread),
        "twin": jnp.asarray(twin),
    }
    scratch = scratch_list()
    names = ["h_" + name for name in INPUTS] + list(OUTS) + [name for name, _ in scratch]
    shapes = [jax.ShapeDtypeStruct((T, KB * DB), BF)] * 2
    shapes += [jax.ShapeDtypeStruct((count, 16, lanes), F32) for _, count, lanes in GROUPS]

    def body(*refs):
        kernel(scale, names, *refs)

    mixed, gtok, left, dright, dleft, gright, uright = pl.pallas_call(
        body,
        out_shape=shapes,
        in_specs=[pl.BlockSpec(memory_space=pl.ANY)] * len(INPUTS),
        out_specs=[pl.BlockSpec(memory_space=pltpu.VMEM)] * len(OUTS),
        scratch_shapes=[shape for _, shape in scratch],
        compiler_params=pltpu.CompilerParams(
            collective_id=0, has_side_effects=True, vmem_limit_bytes=58 * 1024 * 1024
        ),
        name="monarch",
    )(*[given[name] for name in INPUTS])

    left = jnp.transpose(left[:, :MS, :], (1, 0, 2))
    dright = jnp.transpose(dright[:, :MS, :], (1, 0, 2))
    dleft = dleft.reshape(2, 2, 8, DB).transpose(2, 0, 1, 3).reshape(8, KB, DB)

    def unpack(right):
        return right.reshape(2, 8, 2, MB).transpose(1, 0, 2, 3).reshape(8, KB, MB)

    return (
        mixed,
        gtok,
        unpack(gright),
        left[:, :, :MB],
        unpack(uright),
        left[:, :, MB:],
        dright,
        dleft,
    )


def solution(mesh):
    weight = P(None, "blk", None)
    grad = P("dp", "blk", None)
    return jax.shard_map(
        local,
        mesh=mesh,
        in_specs=(P("dp", "blk"),) + (weight,) * 6 + (P("dp", "blk"),),
        out_specs=(P("dp", "blk"),) * 2 + (grad,) * 6,
        check_vma=False,
    )
```

```python
import types

import jax
import jax.numpy as jnp
import numpy as np
from jax import lax
from jax.experimental import pallas as pl
from jax.experimental.pallas import tpu as pltpu
from jax.sharding import PartitionSpec as P

BF = jnp.bfloat16
F32 = jnp.float32
MESH = pl.DeviceIdType.MESH

NB = 32
KB = 4
DB = 256
MB = 448
MS = 14
T = 128
VMEM_LIMIT = 60 * 1024 * 1024
X, Z, Y = 4, 4, 4
OFFS = ((0, 1), (1, 1), (3, 1), (2, 1), (1, 0), (3, 0), (2, 0))


def permutations():
    take = np.zeros((224, 224), np.float32)
    meet = np.zeros((224, 224), np.float32)
    back = np.zeros((224, 224), np.float32)
    for k in range(4):
        for h in range(2):
            for j in range(2):
                for r in range(MS):
                    take[((h * 4 + k) * 2 + j) * MS + r, ((k * 2 + h) * 2 + j) * MS + r] = 1.0
                    meet[((j * 2 + h) * 4 + k) * MS + r, ((h * 4 + k) * 2 + j) * MS + r] = 1.0
                    back[((k * 2 + h) * 2 + j) * MS + r, ((h * 2 + j) * 4 + k) * MS + r] = 1.0
    turn = np.zeros((448, 448), np.float32)
    for p in range(8):
        for h in range(2):
            for i in range(2 * MS):
                turn[h * 224 + p * 28 + i, p * 56 + h * 28 + i] = 1.0
    spread = np.zeros((2, 256, 448), np.float32)
    order = np.zeros((2, 128, 256), np.float32)
    twin = np.zeros((2, 2, 256, 256), np.float32)
    for c in range(2):
        for x in range(X):
            for z in range(Z):
                d = z * 8 + x * 2 + c
                for i in range(MS):
                    spread[c, (x * 4 + z) * 16 + i, d * MS + i] = 1.0
                for i in range(8):
                    order[c, (x * 4 + z) * 8 + i, d * 8 + i] = 1.0
                    for q in range(2):
                        twin[q, c, (x * 4 + z) * 16 + q * 8 + i, d * 8 + i] = 1.0
    out = {
        "take": take,
        "meet": meet,
        "back": back,
        "turn": turn,
        "spread": spread.reshape(512, 448),
        "order": order.reshape(256, 256),
        "twin": twin.reshape(2, 512, 256),
    }
    return {name: np.asarray(value, jnp.bfloat16) for name, value in out.items()}


def untangle():
    out = np.zeros((2, 256, 448), np.float32)
    for h in range(2):
        for p in range(8):
            for i in range(2 * MS):
                out[h, p * 28 + i, p * 56 + h * 28 + i] = 1.0
    return out


def nn(a, b):
    return lax.dot_general(a, b, (((1,), (0,)), ((), ())), preferred_element_type=F32)


def nt(a, b):
    return lax.dot_general(a, b, (((1,), (1,)), ((), ())), preferred_element_type=F32)


def tn(a, b):
    return lax.dot_general(a, b, (((0,), (0,)), ((), ())), preferred_element_type=F32)


INPUTS = (
    "x",
    "wgr",
    "wur",
    "take",
    "wdl",
    "g",
    "wgl",
    "wul",
    "wdr",
    "meet",
    "order",
    "turn",
    "back",
    "spread",
    "twin",
)
SHAPES = {
    "x": (T, KB * DB),
    "g": (T, KB * DB),
    "wgr": (KB, MB, DB),
    "wur": (KB, MB, DB),
    "wdl": (DB, KB, DB),
    "wgl": (MB, KB, MB),
    "wul": (MB, KB, MB),
    "wdr": (MB, KB, DB),
    "take": (224, 224),
    "meet": (224, 224),
    "back": (224, 224),
    "turn": (448, 448),
    "spread": (512, 448),
    "order": (256, 256),
    "twin": (2, 512, 256),
}
GROUPS = (
    ("left", 4, 896),
    ("dright", 4, 256),
    ("dleft", 2, 256),
    ("right0", 1, 896),
    ("right1", 1, 896),
)
UNPACKED = ("left", "dright", "dleft", "right0", "right1", "columns")
OUTS = ("mixed", "gtok") + tuple("o_" + name for name, _, _ in GROUPS)
SLABS = (
    ("a0", (112, 256)),
    ("a1", (112, 256)),
    ("d0", (112, 256)),
    ("d1", (112, 256)),
    ("b0", (64, T)),
    ("b1", (64, T)),
    ("c", (128, T)),
)


def scratch_list():
    out = []

    def add(name, shape, dtype=BF):
        out.append((name, pltpu.VMEM(shape, dtype)))

    for name in INPUTS:
        add("v_" + name, SHAPES[name])
    out.append(("in_sem", pltpu.SemaphoreType.DMA((len(INPUTS),))))
    for name, slab in SLABS:
        add("s_" + name, (8,) + slab)
        add("r_" + name, (8,) + slab)
        out.append(("ss_" + name, pltpu.SemaphoreType.DMA((7,))))
        out.append(("rs_" + name, pltpu.SemaphoreType.DMA((7,))))
    add("gl", (KB, MB, MB))
    add("ul", (KB, MB, MB))
    add("dr", (KB, DB, MB))
    add("dl", (KB, DB, DB))
    add("turned_g", (KB, 2, 224, DB))
    add("turned_u", (KB, 2, 224, DB))
    add("flow", (KB, MB, 2 * T), F32)
    add("seen", (KB, Y, 112, 2 * T))
    add("back32", (KB, Y, 56, 2 * T), F32)
    add("back", (KB, 224, 2 * T))
    add("act", (KB, T, MB), F32)
    add("slope", (KB, T, MB), F32)
    add("hidden", (KB, T, MB))
    add("dback32", (KB, 8, 4, 8, T), F32)
    add("dseen32", (KB, 8, 4, 8, T), F32)
    add("dback", (KB, DB, T))
    add("dseen", (KB, DB, T))
    add("lhs_left", (KB, 2, 256, 256))
    add("rhs_left", (KB, 256, 896))
    add("lhs_dright", (KB, 2, 256, T))
    add("lhs_dleft", (2, 2, 256, 256))
    add("lhs_right", (2, 128, 512))
    add("rhs_gright", (896, 512))
    add("rhs_uright", (896, 512))
    add("tok", (T, KB * DB), F32)
    for name, count, lanes in GROUPS:
        add("s0_" + name, (count, 256, lanes))
        add("r0_" + name, (count, 256, lanes))
        add("s1_" + name, (count, X, 64, lanes))
        add("r1_" + name, (count, 3, 64, lanes))
        add("s2_" + name, (count, Z, 16, lanes))
        add("r2_" + name, (3, count, 16, lanes))
        for kind in ("ss0_", "rs0_"):
            out.append((kind + name, pltpu.SemaphoreType.DMA((count,))))
        for kind in ("ss1_", "rs1_"):
            out.append((kind + name, pltpu.SemaphoreType.DMA((count * 3,))))
        for kind in ("ss2_", "rs2_"):
            out.append((kind + name, pltpu.SemaphoreType.DMA((3,))))
    return out


def loop(count, body):
    lax.fori_loop(0, count, lambda i, _: (body(i), 0)[1], 0)


def kernel(scale, names, *refs):
    r = types.SimpleNamespace(**dict(zip(names, refs)))
    v = vars(r)
    dp = lax.axis_index("dp")
    blk = lax.axis_index("blk")
    core, x, z = dp % 2, (dp // 2) % X, dp // 8
    y, zh = blk // 2, blk % 2
    pending = []

    loads = {}
    for i, name in enumerate(INPUTS):
        loads[name] = pltpu.make_async_copy(v["h_" + name], v["v_" + name], r.in_sem.at[i])
        loads[name].start()

    def need(*which):
        for name in which:
            loads[name].wait()

    def blk_peer(dy, dz):
        return ((y + dy) % Y) * 2 + (zh + dz) % 2

    def dp_id(z_, x_, c_):
        return (z_ * 8 + x_ * 2 + c_, blk)

    core_id = dp_id(z, x, 1 - core)
    x_ids = [dp_id(z, (x + d) % X, core) for d in (1, 2, 3)]
    z_ids = [dp_id((z + d) % Z, x, core) for d in (1, 2, 3)]
    everyone = [(dp, blk_peer(dy, dz)) for dy, dz in OFFS] + [core_id] + x_ids + z_ids

    barrier = pltpu.get_barrier_semaphore()
    for who in everyone:
        pl.semaphore_signal(barrier, inc=1, device_id=who, device_id_type=MESH)

    def remote(src, dst, ss, rs, who):
        copy = pltpu.make_async_remote_copy(
            src_ref=src, dst_ref=dst, send_sem=ss, recv_sem=rs, device_id=who, device_id_type=MESH
        )
        copy.start()
        pending.append(copy)
        return copy

    def exchange(name):
        s, d, ss, rs = (v[k + name] for k in ("s_", "r_", "ss_", "rs_"))
        out = {}
        for i, (dy, dz) in enumerate(OFFS):
            p = blk_peer(dy, dz)
            out[dy, dz] = remote(s.at[p], d.at[blk], ss.at[i], rs.at[i], (dp, p))
        d[blk] = s[blk]
        return out

    def pairs(name, copies, matrix, use):
        for dy in range(4):
            for dz in range(2):
                if (dy, dz) != (0, 0):
                    copies[dy, dz].wait_recv()
            ys = (y - dy + Y) % Y
            two = v["r_" + name][pl.ds(ys * 2, 2)].reshape(224, 2 * T)
            use(ys, nn(matrix[...], two))

    def unswap(source, wide, out):
        def one(s):
            got = source(s).astype(F32).reshape(4, 4, 8, T)
            for a in range(4):
                for b in range(4):
                    wide[b, s, a] = got[a, b]

        loop(8, one)
        for b in range(KB):
            out[b] = wide[b].reshape(DB, T).astype(BF)

    def arrived(copies):
        for copy in copies.values():
            copy.wait_recv()

    def sent(copies):
        for copy in copies.values():
            copy.wait_send()
        gone = {id(copy) for copy in copies.values()}
        pending[:] = [copy for copy in pending if id(copy) not in gone]

    need("x", "wgr", "wur", "take")
    for k in range(KB):
        xk = r.v_x[:, k * DB : (k + 1) * DB]
        r.flow[k, :, :T] = nt(r.v_wgr[k], xk)
        r.flow[k, :, T:] = nt(r.v_wur[k], xk)
    for p in range(8):
        rows = r.flow[:, p * 56 : (p + 1) * 56, :].reshape(224, 2 * T).astype(BF)
        taken = nn(r.v_take[...], rows).astype(BF)
        r.s_a0[p] = taken[:112]
        r.s_a1[p] = taken[112:]
    pl.semaphore_wait(barrier, len(everyone))
    from_a = [exchange("a0")]

    need("wdl", "g")
    r.dl[...] = jnp.swapaxes(r.v_wdl[...], 0, 1)
    for j in range(KB):
        f = nt(r.dl[j], r.v_g[:, j * DB : (j + 1) * DB]).astype(BF)
        r.s_c[:, j * 32 : (j + 1) * 32, :] = f.reshape(8, 32, T)

    need("wgl", "wul", "wdr", "meet", "order", "turn", "back", "spread", "twin")
    r.gl[...] = jnp.swapaxes(r.v_wgl[...], 0, 1)
    r.ul[...] = jnp.swapaxes(r.v_wul[...], 0, 1)
    eye = lax.broadcasted_iota(jnp.int32, (DB, DB), 0) == lax.broadcasted_iota(jnp.int32, (DB, DB), 1)
    eye = eye.astype(F32).astype(BF)
    swapped = jnp.swapaxes(r.v_wdr[...], 0, 1)
    for k in range(KB):
        r.dr[k] = nt(eye, swapped[k]).astype(BF)
    r.rhs_gright[...] = jnp.zeros_like(r.rhs_gright)
    r.rhs_uright[...] = jnp.zeros_like(r.rhs_uright)
    for k in range(KB):
        f = nt(r.v_order[...], r.v_x[:, k * DB : (k + 1) * DB]).astype(BF)
        r.lhs_right[:, :, k * T : (k + 1) * T] = f.reshape(2, 128, T)

    def turned(k):
        r.turned_g[k] = nn(r.v_turn[...], r.v_wgr[k]).astype(BF).reshape(2, 224, DB)
        r.turned_u[k] = nn(r.v_turn[...], r.v_wur[k]).astype(BF).reshape(2, 224, DB)

    loop(KB, turned)

    def forward(h):
        def keep(ys, moved):
            r.seen[2 * h : 2 * h + 2, pl.ds(ys, 1)] = moved.astype(BF).reshape(2, 1, 112, 2 * T)

        pairs("a%d" % h, from_a[h], r.v_meet, keep)
        for i in range(2):
            j = 2 * h + i
            seen = r.seen[j].reshape(MB, 2 * T)
            pre = tn(seen[:, :T], r.gl[j])
            up = tn(seen[:, T:], r.ul[j])
            sig = jax.nn.sigmoid(pre)
            act = pre * sig
            hidden = (act * up).astype(BF)
            r.act[j] = act
            r.slope[j] = up * sig * (1.0 + pre * (1.0 - sig))
            r.hidden[j] = hidden
            f = nt(r.dr[j], hidden).astype(BF)
            v["s_b%d" % h][:, i * 32 : (i + 1) * 32, :] = f.reshape(8, 32, T)

    def backward(h):
        for i in range(2):
            j = 2 * h + i
            hf = tn(r.dback[j], r.dr[j])
            gg = (hf * r.slope[j]).astype(BF)
            ug = (hf * r.act[j]).astype(BF)
            r.flow[i, :, :T] = nt(r.gl[j], gg)
            r.flow[i, :, T:] = nt(r.ul[j], ug)
            r.rhs_left[j, :T, :] = jnp.concatenate([gg, jnp.zeros((T, MB), BF)], axis=1)
            r.rhs_left[j, T:, :] = jnp.concatenate([jnp.zeros((T, MB), BF), ug], axis=1)
        for p in range(8):
            rows = r.flow[:2, p * 56 : (p + 1) * 56, :].reshape(112, 2 * T)
            v["s_d%d" % h][p] = rows.astype(BF)

    moves = {}

    def start_core(name, which, half):
        s0, r0, ss, rs = (v[k + name] for k in ("s0_", "r0_", "ss0_", "rs0_"))
        for j in which:
            s0[j] = half(j, 1 - core).astype(BF)
            moves[name, 0, j] = remote(s0.at[j], r0.at[j], ss.at[j], rs.at[j], core_id)

    def start_x(name, which, half):
        r0, s1, r1, ss, rs = (v[k + name] for k in ("r0_", "s1_", "r1_", "ss1_", "rs1_"))
        for j in which:
            own = half(j, core)
            moves[name, 0, j].wait_recv()
            s1[j] = (own + r0[j].astype(F32)).astype(BF).reshape(s1.shape[1:])
            for i in (0, 2, 1):
                moves[name, 1, j, i] = remote(
                    s1.at[j, (x + i + 1) % X],
                    r1.at[j, i],
                    ss.at[j * 3 + i],
                    rs.at[j * 3 + i],
                    x_ids[i],
                )

    def start_z(name, count):
        s1, r1, s2, r2, ss, rs = (
            v[k + name] for k in ("s1_", "r1_", "s2_", "r2_", "ss2_", "rs2_")
        )
        for j in range(count):
            for i in range(3):
                moves[name, 1, j, i].wait_recv()
            total = s1[j, x].astype(F32)
            for i in range(3):
                total = total + r1[j, i].astype(F32)
            s2[j] = total.astype(BF).reshape(s2.shape[1:])
        for i in range(3):
            moves[name, 2, i] = remote(
                s2.at[:, (z + i + 1) % Z], r2.at[i], ss.at[i], rs.at[i], z_ids[i]
            )

    def finish(name, count):
        s2, r2, out = v["s2_" + name], v["r2_" + name], v["o_" + name]
        for i in range(3):
            moves[name, 2, i].wait_recv()
        for j in range(count):
            total = s2[j, z].astype(F32)
            for i in range(3):
                total = total + r2[i, j].astype(F32)
            out[j] = scale * total

    def sides(h):
        for j in (2 * h, 2 * h + 1):
            f = nn(r.v_spread[...], r.seen[j].reshape(MB, 2 * T)).astype(BF)
            r.lhs_left[j] = f.reshape(2, 256, 2 * T)
            f = nt(r.v_spread[...], r.hidden[j]).astype(BF)
            r.lhs_dright[j] = f.reshape(2, 256, T)

    def left_half(j, c):
        return nn(r.lhs_left[j, c], r.rhs_left[j])

    def dright_half(j, c):
        return nt(r.lhs_dright[j, c], r.dback[j])

    def dleft_half(q, c):
        rows = [r.v_g[:, (2 * q + i) * DB : (2 * q + i + 1) * DB] for i in range(2)]
        return nn(r.lhs_dleft[q, c], jnp.concatenate(rows, axis=0))

    def right_half(j, c):
        both = [nt(r.lhs_right[c], rhs[...]) for rhs in (r.rhs_gright, r.rhs_uright)]
        both = [part.reshape(16, 1, 8, 896) for part in both]
        return jnp.concatenate(both, axis=1).reshape(256, 896)

    def token_part(h, k):
        part = tn(r.back[k, :, :T], r.turned_g[k, h])
        return part + tn(r.back[k, :, T:], r.turned_u[k, h])

    def right(h):
        def keep(ys, moved):
            r.back32[:, pl.ds(ys, 1)] = moved.reshape(KB, 1, 56, 2 * T)

        pairs("d%d" % h, from_d[h], r.v_back, keep)
        for k in range(KB):
            back = r.back32[k].reshape(224, 2 * T).astype(BF)
            r.back[k] = back
            r.rhs_gright[k * 224 : (k + 1) * 224, k * T : (k + 1) * T] = back[:, :T]
            r.rhs_uright[k * 224 : (k + 1) * 224, k * T : (k + 1) * T] = back[:, T:]
        start_core("right%d" % h, (0,), right_half)

    def left(h):
        which = (2 * h, 2 * h + 1)
        sides(h)
        start_core("left", which, left_half)
        start_core("dright", which, dright_half)
        start_x("left", which, left_half)
        start_x("dright", which, dright_half)

    sent(from_a[0])
    from_c = exchange("c")
    forward(0)
    sent(from_c)
    from_a.append(exchange("a1"))
    arrived(from_c)
    unswap(lambda s: r.r_c[s], r.dback32, r.dback)
    backward(0)
    left(0)
    sent(from_a[1])
    from_d = [exchange("d0")]
    forward(1)
    backward(1)
    left(1)
    sent(from_d[0])
    from_d.append(exchange("d1"))

    right(0)
    for k in range(KB):
        r.tok[:, k * DB : (k + 1) * DB] = token_part(0, k)
    start_x("right0", (0,), right_half)
    sent(from_d[1])
    from_b = [exchange("b0"), exchange("b1")]

    right(1)
    start_x("right1", (0,), right_half)
    start_z("left", 4)
    start_z("dright", 4)
    start_z("right0", 1)

    for copies in from_b:
        arrived(copies)
    unswap(lambda s: jnp.concatenate([r.r_b0[s], r.r_b1[s]], axis=0), r.dseen32, r.dseen)
    for j in range(KB):
        f = nn(r.v_twin[j % 2], r.dseen[j]).astype(BF)
        r.lhs_dleft[j // 2, :, :, (j % 2) * T : (j % 2 + 1) * T] = f.reshape(2, 256, T)
    start_core("dleft", (0, 1), dleft_half)
    start_x("dleft", (0, 1), dleft_half)
    for k in range(KB):
        columns = slice(k * DB, (k + 1) * DB)
        r.gtok[:, columns] = (r.tok[:, columns] + token_part(1, k)).astype(BF)
    start_z("right1", 1)
    for j in range(KB):
        r.mixed[:, j * DB : (j + 1) * DB] = tn(r.dseen[j], r.dl[j]).astype(BF)
    start_z("dleft", 2)
    finish("left", 4)
    finish("dright", 4)
    finish("right0", 1)
    finish("right1", 1)
    finish("dleft", 2)
    for copy in pending:
        copy.wait_send()


def unpack(names, *refs):
    r = types.SimpleNamespace(**dict(zip(names, refs)))
    copies = [
        pltpu.make_async_copy(r.mixed_in, r.mixed, r.sem.at[0]),
        pltpu.make_async_copy(r.gtok_in, r.gtok, r.sem.at[1]),
    ]
    for i, name in enumerate(UNPACKED):
        copies.append(pltpu.make_async_copy(vars(r)["h_" + name], vars(r)[name], r.sem.at[2 + i]))
    for copy in copies:
        copy.start()
    for copy in copies[2:]:
        copy.wait()
    total = None
    for h, source in enumerate((r.right0, r.right1)):
        rows = source[0]
        parts = [rows[:, :256]] + [pltpu.roll(rows, 896 - 224 * k, 1)[:, :256] for k in (1, 2, 3)]
        part = lax.dot_general(
            jnp.concatenate(parts, axis=0),
            r.columns[h],
            (((1,), (0,)), ((), ())),
            precision=lax.Precision.HIGHEST,
            preferred_element_type=F32,
        )
        total = part if total is None else total + part
    for k in range(KB):
        r.gr[:, k, :] = total[k * 16 : k * 16 + 8]
        r.ur[:, k, :] = total[k * 16 + 8 : k * 16 + 16]
    for j in range(KB):
        rows = r.left[j]
        r.gl[:, j, :] = rows[:MS, :MB]
        r.ul[:, j, :] = rows[:MS, MB:]
        r.dr[:, j, :] = r.dright[j][:MS]
        r.dl[:, j, :] = r.dleft[j // 2][(j % 2) * 8 : (j % 2 + 1) * 8]
    for copy in copies[:2]:
        copy.wait()


def local(tokens, gate_right, gate_left, upward_right, upward_left, down_right, down_left, cotangent):
    scale = float(tokens.shape[0] * lax.axis_size("dp")) ** (-0.5)
    given = {
        "x": tokens,
        "g": cotangent,
        "wgr": jnp.transpose(gate_right, (1, 2, 0)),
        "wur": jnp.transpose(upward_right, (1, 2, 0)),
        "wdl": down_left,
        "wgl": gate_left,
        "wul": upward_left,
        "wdr": down_right,
    }
    given.update({name: jnp.asarray(value) for name, value in permutations().items()})
    scratch = scratch_list()
    names = ["h_" + name for name in INPUTS] + list(OUTS) + [name for name, _ in scratch]
    shapes = [jax.ShapeDtypeStruct((T, KB * DB), BF)] * 2
    shapes += [jax.ShapeDtypeStruct((count, 16, lanes), F32) for _, count, lanes in GROUPS]

    def body(*refs):
        kernel(scale, names, *refs)

    results = pl.pallas_call(
        body,
        out_shape=shapes,
        in_specs=[pl.BlockSpec(memory_space=pl.ANY)] * len(INPUTS),
        out_specs=[pl.BlockSpec(memory_space=pltpu.VMEM)] * len(OUTS),
        scratch_shapes=[shape for _, shape in scratch],
        compiler_params=pltpu.CompilerParams(
            collective_id=0, has_side_effects=True, vmem_limit_bytes=VMEM_LIMIT
        ),
        name="monarch",
    )(*[given[name] for name in INPUTS])

    last = [
        ((T, KB * DB), BF),
        ((T, KB * DB), BF),
        ((8, KB, MB), F32),
        ((MS, KB, MB), F32),
        ((8, KB, MB), F32),
        ((MS, KB, MB), F32),
        ((MS, KB, DB), F32),
        ((8, KB, DB), F32),
    ]
    anywhere, vmem = pl.BlockSpec(memory_space=pl.ANY), pl.BlockSpec(memory_space=pltpu.VMEM)
    parts = list(results[2:]) + [jnp.asarray(untangle())]
    names = ["mixed_in", "gtok_in"] + ["h_" + name for name in UNPACKED]
    names += ["mixed", "gtok", "gr", "gl", "ur", "ul", "dr", "dl"] + list(UNPACKED) + ["sem"]
    return pl.pallas_call(
        lambda *refs: unpack(names, *refs),
        out_shape=[jax.ShapeDtypeStruct(*entry) for entry in last],
        in_specs=[anywhere] * (2 + len(parts)),
        out_specs=[vmem] * 8,
        scratch_shapes=[pltpu.VMEM(part.shape, F32) for part in parts]
        + [pltpu.SemaphoreType.DMA((2 + len(parts),))],
        compiler_params=pltpu.CompilerParams(vmem_limit_bytes=VMEM_LIMIT),
        name="unpack",
    )(*results[:2], *parts)


def solution(mesh):
    weight = P(None, "blk", None)
    grad = P("dp", "blk", None)
    return jax.shard_map(
        local,
        mesh=mesh,
        in_specs=(P("dp", "blk"),) + (weight,) * 6 + (P("dp", "blk"),),
        out_specs=(P("dp", "blk"),) * 2 + (grad,) * 6,
        check_vma=False,
    )
```

```python
import types

import jax
import jax.numpy as jnp
import numpy as np
from jax import lax
from jax.experimental import pallas as pl
from jax.experimental.pallas import tpu as pltpu
from jax.sharding import PartitionSpec as P

BF = jnp.bfloat16
F32 = jnp.float32
MESH = pl.DeviceIdType.MESH

NB = 32
KB = 4
DB = 256
MB = 448
MS = 14
T = 128
VMEM_LIMIT = 60 * 1024 * 1024
X, Z, Y = 4, 4, 4
OFFS = ((0, 1), (1, 1), (3, 1), (2, 1), (1, 0), (3, 0), (2, 0))


def permutations():
    take = np.zeros((224, 224), np.float32)
    meet = np.zeros((224, 224), np.float32)
    back = np.zeros((224, 224), np.float32)
    for k in range(4):
        for h in range(2):
            for j in range(2):
                for r in range(MS):
                    take[((h * 4 + k) * 2 + j) * MS + r, ((k * 2 + h) * 2 + j) * MS + r] = 1.0
                    meet[((j * 2 + h) * 4 + k) * MS + r, ((h * 4 + k) * 2 + j) * MS + r] = 1.0
                    back[((k * 2 + h) * 2 + j) * MS + r, ((h * 2 + j) * 4 + k) * MS + r] = 1.0
    turn = np.zeros((448, 448), np.float32)
    for p in range(8):
        for h in range(2):
            for i in range(2 * MS):
                turn[h * 224 + p * 28 + i, p * 56 + h * 28 + i] = 1.0
    spread = np.zeros((2, 256, 448), np.float32)
    order = np.zeros((2, 128, 256), np.float32)
    twin = np.zeros((2, 2, 256, 256), np.float32)
    for c in range(2):
        for x in range(X):
            for z in range(Z):
                d = z * 8 + x * 2 + c
                for i in range(MS):
                    spread[c, (x * 4 + z) * 16 + i, d * MS + i] = 1.0
                for i in range(8):
                    order[c, (x * 4 + z) * 8 + i, d * 8 + i] = 1.0
                    for q in range(2):
                        twin[q, c, (x * 4 + z) * 16 + q * 8 + i, d * 8 + i] = 1.0
    out = {
        "take": take,
        "meet": meet,
        "back": back,
        "turn": turn,
        "spread": spread.reshape(512, 448),
        "order": order.reshape(256, 256),
        "twin": twin.reshape(2, 512, 256),
    }
    return {name: np.asarray(value, jnp.bfloat16) for name, value in out.items()}


def untangle():
    out = np.zeros((2, 256, 448), np.float32)
    for h in range(2):
        for p in range(8):
            for i in range(2 * MS):
                out[h, p * 28 + i, p * 56 + h * 28 + i] = 1.0
    return out


def nn(a, b):
    return lax.dot_general(a, b, (((1,), (0,)), ((), ())), preferred_element_type=F32)


def nt(a, b):
    return lax.dot_general(a, b, (((1,), (1,)), ((), ())), preferred_element_type=F32)


def tn(a, b):
    return lax.dot_general(a, b, (((0,), (0,)), ((), ())), preferred_element_type=F32)


INPUTS = (
    "x",
    "wgr",
    "wur",
    "take",
    "wdl",
    "g",
    "wgl",
    "wul",
    "wdr",
    "meet",
    "order",
    "turn",
    "back",
    "spread",
    "twin",
)
FIRST = 4
SHAPES = {
    "x": (T, KB * DB),
    "g": (T, KB * DB),
    "wgr": (KB, MB, DB),
    "wur": (KB, MB, DB),
    "wdl": (DB, KB, DB),
    "wgl": (MB, KB, MB),
    "wul": (MB, KB, MB),
    "wdr": (MB, KB, DB),
    "take": (224, 224),
    "meet": (224, 224),
    "back": (224, 224),
    "turn": (448, 448),
    "spread": (512, 448),
    "order": (256, 256),
    "twin": (2, 512, 256),
}
GROUPS = (
    ("left0", 2, 896),
    ("left1", 2, 896),
    ("dright0", 2, 256),
    ("dright1", 2, 256),
    ("dleft", 2, 256),
    ("right0", 1, 896),
    ("right1", 1, 896),
)
PAIRED = ("left0", "left1", "dright0", "dright1")
UNPACKED = PAIRED + ("dleft", "right0", "right1", "columns")
OUTS = ("mixed", "gtok") + tuple("o_" + name for name, _, _ in GROUPS)
SLABS = (
    ("a0", (112, 256)),
    ("a1", (112, 256)),
    ("d0", (112, 256)),
    ("d1", (112, 256)),
    ("b0", (64, T)),
    ("b1", (64, T)),
    ("c", (128, T)),
)


def scratch_list():
    out = []

    def add(name, shape, dtype=BF):
        out.append((name, pltpu.VMEM(shape, dtype)))

    for name in INPUTS:
        add("v_" + name, SHAPES[name])
    out.append(("in_sem", pltpu.SemaphoreType.DMA((len(INPUTS),))))
    for name, slab in SLABS:
        add("s_" + name, (8,) + slab)
        add("r_" + name, (8,) + slab)
        out.append(("ss_" + name, pltpu.SemaphoreType.DMA((7,))))
        out.append(("rs_" + name, pltpu.SemaphoreType.DMA((7,))))
    add("gl", (KB, MB, MB))
    add("ul", (KB, MB, MB))
    add("dr", (KB, DB, MB))
    add("dl", (KB, DB, DB))
    add("turned_g", (KB, 2, 224, DB))
    add("turned_u", (KB, 2, 224, DB))
    add("flow", (KB, MB, 2 * T), F32)
    add("seen", (KB, Y, 112, 2 * T))
    add("back32", (KB, Y, 56, 2 * T), F32)
    add("back", (KB, 224, 2 * T))
    add("act", (KB, T, MB), F32)
    add("slope", (KB, T, MB), F32)
    add("hidden", (KB, T, MB))
    add("dback32", (KB, 8, 4, 8, T), F32)
    add("dseen32", (KB, 8, 4, 8, T), F32)
    add("dback", (KB, DB, T))
    add("dseen", (KB, DB, T))
    add("lhs_left", (KB, 2, 256, 256))
    add("rhs_left", (KB, 256, 896))
    add("lhs_dright", (KB, 2, 256, T))
    add("lhs_dleft", (2, 2, 256, 256))
    add("lhs_right", (2, 128, 512))
    add("rhs_gright", (896, 512))
    add("rhs_uright", (896, 512))
    add("tok", (T, KB * DB), F32)
    for name, count, lanes in GROUPS:
        add("s0_" + name, (count, 256, lanes))
        add("r0_" + name, (count, 256, lanes))
        add("s1_" + name, (count, X, 64, lanes))
        add("r1_" + name, (count, 3, 64, lanes))
        if name in PAIRED:
            add("s2_" + name, (count, 2, 2, 16, lanes))
            add("r2_" + name, (count, 2, 16, lanes))
            add("s3_" + name, (count, 2, 16, lanes))
            add("r3_" + name, (count, 16, lanes))
        else:
            add("s2_" + name, (count, Z, 16, lanes))
            add("r2_" + name, (3, count, 16, lanes))
        for kind in ("ss0_", "rs0_"):
            out.append((kind + name, pltpu.SemaphoreType.DMA((count,))))
        for kind in ("ss1_", "rs1_"):
            out.append((kind + name, pltpu.SemaphoreType.DMA((count * 3,))))
        for kind in ("ss2_", "rs2_"):
            out.append((kind + name, pltpu.SemaphoreType.DMA((3,))))
    return out


def loop(count, body):
    lax.fori_loop(0, count, lambda i, _: (body(i), 0)[1], 0)


def kernel(scale, names, *refs):
    r = types.SimpleNamespace(**dict(zip(names, refs)))
    v = vars(r)
    dp = lax.axis_index("dp")
    blk = lax.axis_index("blk")
    core, x, z = dp % 2, (dp // 2) % X, dp // 8
    y, zh = blk // 2, blk % 2
    pending = []

    loads = {}
    for i, name in enumerate(INPUTS):
        loads[name] = pltpu.make_async_copy(v["h_" + name], v["v_" + name], r.in_sem.at[i])

    def load(*which):
        for name in which:
            loads[name].start()

    load(*INPUTS[:FIRST])

    def need(*which):
        for name in which:
            loads[name].wait()

    def blk_peer(dy, dz):
        return ((y + dy) % Y) * 2 + (zh + dz) % 2

    def dp_id(z_, x_, c_):
        return (z_ * 8 + x_ * 2 + c_, blk)

    core_id = dp_id(z, x, 1 - core)
    x_ids = [dp_id(z, (x + d) % X, core) for d in (1, 2, 3)]
    z_ids = [dp_id((z + d) % Z, x, core) for d in (1, 2, 3)]
    everyone = [(dp, blk_peer(dy, dz)) for dy, dz in OFFS] + [core_id] + x_ids + z_ids

    barrier = pltpu.get_barrier_semaphore()
    for who in everyone:
        pl.semaphore_signal(barrier, inc=1, device_id=who, device_id_type=MESH)

    def remote(src, dst, ss, rs, who):
        copy = pltpu.make_async_remote_copy(
            src_ref=src, dst_ref=dst, send_sem=ss, recv_sem=rs, device_id=who, device_id_type=MESH
        )
        copy.start()
        pending.append(copy)
        return copy

    def exchange(name):
        s, d, ss, rs = (v[k + name] for k in ("s_", "r_", "ss_", "rs_"))
        out = {}
        for i, (dy, dz) in enumerate(OFFS):
            p = blk_peer(dy, dz)
            out[dy, dz] = remote(s.at[p], d.at[blk], ss.at[i], rs.at[i], (dp, p))
        d[blk] = s[blk]
        return out

    def pairs(name, copies, matrix, use):
        for dy in range(4):
            for dz in range(2):
                if (dy, dz) != (0, 0):
                    copies[dy, dz].wait_recv()
            ys = (y - dy + Y) % Y
            two = v["r_" + name][pl.ds(ys * 2, 2)].reshape(224, 2 * T)
            use(ys, nn(matrix[...], two))

    def unswap(source, wide, out):
        def one(s):
            got = source(s).astype(F32).reshape(4, 4, 8, T)
            for a in range(4):
                for b in range(4):
                    wide[b, s, a] = got[a, b]

        loop(8, one)
        for b in range(KB):
            out[b] = wide[b].reshape(DB, T).astype(BF)

    def arrived(copies):
        for copy in copies.values():
            copy.wait_recv()

    def sent(copies):
        for copy in copies.values():
            copy.wait_send()
        gone = {id(copy) for copy in copies.values()}
        pending[:] = [copy for copy in pending if id(copy) not in gone]

    need(*INPUTS[:FIRST])
    load(*INPUTS[FIRST:])
    for k in range(KB):
        xk = r.v_x[:, k * DB : (k + 1) * DB]
        r.flow[k, :, :T] = nt(r.v_wgr[k], xk)
        r.flow[k, :, T:] = nt(r.v_wur[k], xk)
    for p in range(8):
        rows = r.flow[:, p * 56 : (p + 1) * 56, :].reshape(224, 2 * T).astype(BF)
        taken = nn(r.v_take[...], rows).astype(BF)
        r.s_a0[p] = taken[:112]
        r.s_a1[p] = taken[112:]
    pl.semaphore_wait(barrier, len(everyone))
    from_a = [exchange("a0")]

    need("wdl", "g")
    r.dl[...] = jnp.swapaxes(r.v_wdl[...], 0, 1)
    for j in range(KB):
        f = nt(r.dl[j], r.v_g[:, j * DB : (j + 1) * DB]).astype(BF)
        r.s_c[:, j * 32 : (j + 1) * 32, :] = f.reshape(8, 32, T)

    need("wgl", "wul", "wdr", "meet", "order", "turn", "back", "spread", "twin")
    r.gl[...] = jnp.swapaxes(r.v_wgl[...], 0, 1)
    r.ul[...] = jnp.swapaxes(r.v_wul[...], 0, 1)
    eye = lax.broadcasted_iota(jnp.int32, (DB, DB), 0) == lax.broadcasted_iota(jnp.int32, (DB, DB), 1)
    eye = eye.astype(F32).astype(BF)
    swapped = jnp.swapaxes(r.v_wdr[...], 0, 1)
    for k in range(KB):
        r.dr[k] = nt(eye, swapped[k]).astype(BF)
    r.rhs_gright[...] = jnp.zeros_like(r.rhs_gright)
    r.rhs_uright[...] = jnp.zeros_like(r.rhs_uright)
    for k in range(KB):
        f = nt(r.v_order[...], r.v_x[:, k * DB : (k + 1) * DB]).astype(BF)
        r.lhs_right[:, :, k * T : (k + 1) * T] = f.reshape(2, 128, T)

    def turned(k):
        r.turned_g[k] = nn(r.v_turn[...], r.v_wgr[k]).astype(BF).reshape(2, 224, DB)
        r.turned_u[k] = nn(r.v_turn[...], r.v_wur[k]).astype(BF).reshape(2, 224, DB)

    loop(KB, turned)

    def forward(h):
        def keep(ys, moved):
            r.seen[2 * h : 2 * h + 2, pl.ds(ys, 1)] = moved.astype(BF).reshape(2, 1, 112, 2 * T)

        pairs("a%d" % h, from_a[h], r.v_meet, keep)
        for i in range(2):
            j = 2 * h + i
            seen = r.seen[j].reshape(MB, 2 * T)
            pre = tn(seen[:, :T], r.gl[j])
            up = tn(seen[:, T:], r.ul[j])
            sig = jax.nn.sigmoid(pre)
            act = pre * sig
            hidden = (act * up).astype(BF)
            r.act[j] = act
            r.slope[j] = up * sig * (1.0 + pre * (1.0 - sig))
            r.hidden[j] = hidden
            f = nt(r.dr[j], hidden).astype(BF)
            v["s_b%d" % h][:, i * 32 : (i + 1) * 32, :] = f.reshape(8, 32, T)

    def backward(h):
        for i in range(2):
            j = 2 * h + i
            hf = tn(r.dback[j], r.dr[j])
            gg = (hf * r.slope[j]).astype(BF)
            ug = (hf * r.act[j]).astype(BF)
            r.flow[i, :, :T] = nt(r.gl[j], gg)
            r.flow[i, :, T:] = nt(r.ul[j], ug)
            r.rhs_left[j, :T, :] = jnp.concatenate([gg, jnp.zeros((T, MB), BF)], axis=1)
            r.rhs_left[j, T:, :] = jnp.concatenate([jnp.zeros((T, MB), BF), ug], axis=1)
        for p in range(8):
            rows = r.flow[:2, p * 56 : (p + 1) * 56, :].reshape(112, 2 * T)
            v["s_d%d" % h][p] = rows.astype(BF)

    moves = {}

    def start_core(name, which, half):
        s0, r0, ss, rs = (v[k + name] for k in ("s0_", "r0_", "ss0_", "rs0_"))
        for j in which:
            s0[j] = half(j, 1 - core).astype(BF)
            moves[name, 0, j] = remote(s0.at[j], r0.at[j], ss.at[j], rs.at[j], core_id)

    def start_x(name, which, half):
        r0, s1, r1, ss, rs = (v[k + name] for k in ("r0_", "s1_", "r1_", "ss1_", "rs1_"))
        for j in which:
            own = half(j, core)
            moves[name, 0, j].wait_recv()
            s1[j] = (own + r0[j].astype(F32)).astype(BF).reshape(s1.shape[1:])
            for i in (0, 2, 1):
                moves[name, 1, j, i] = remote(
                    s1.at[j, (x + i + 1) % X],
                    r1.at[j, i],
                    ss.at[j * 3 + i],
                    rs.at[j * 3 + i],
                    x_ids[i],
                )

    def start_z(name, count):
        s1, r1, s2, r2, ss, rs = (
            v[k + name] for k in ("s1_", "r1_", "s2_", "r2_", "ss2_", "rs2_")
        )
        for j in range(count):
            for i in range(3):
                moves[name, 1, j, i].wait_recv()
            total = s1[j, x].astype(F32)
            for i in range(3):
                total = total + r1[j, i].astype(F32)
            s2[j] = total.astype(BF).reshape(s2.shape[1:])
        for i in range(3):
            moves[name, 2, i] = remote(
                s2.at[:, (z + i + 1) % Z], r2.at[i], ss.at[i], rs.at[i], z_ids[i]
            )

    def start_pair(name, count):
        s1, r1, s2, r2, ss, rs = (
            v[k + name] for k in ("s1_", "r1_", "s2_", "r2_", "ss2_", "rs2_")
        )
        for j in range(count):
            for i in range(3):
                moves[name, 1, j, i].wait_recv()
            total = s1[j, x].astype(F32)
            for i in range(3):
                total = total + r1[j, i].astype(F32)
            s2[j] = total.astype(BF).reshape(s2.shape[1:])
        near = z + 1 - 2 * (z % 2)
        moves[name, 2] = remote(
            s2.at[:, :, 1 - z % 2], r2, ss.at[0], rs.at[0], dp_id(near, x, core)
        )

    def start_far(name, count):
        s2, r2, s3, r3, ss, rs = (
            v[k + name] for k in ("s2_", "r2_", "s3_", "r3_", "ss2_", "rs2_")
        )
        moves[name, 2].wait_recv()
        for j in range(count):
            for i in range(2):
                s3[j, i] = (s2[j, i, z % 2].astype(F32) + r2[j, i].astype(F32)).astype(BF)
        moves[name, 3] = remote(
            s3.at[:, 1 - z // 2], r3, ss.at[1], rs.at[1], dp_id((z + 2) % Z, x, core)
        )

    def finish_far(name, count):
        s3, r3, out = v["s3_" + name], v["r3_" + name], v["o_" + name]
        moves[name, 3].wait_recv()
        for j in range(count):
            out[j] = scale * (s3[j, z // 2].astype(F32) + r3[j].astype(F32))

    def finish(name, count):
        s2, r2, out = v["s2_" + name], v["r2_" + name], v["o_" + name]
        for i in range(3):
            moves[name, 2, i].wait_recv()
        for j in range(count):
            total = s2[j, z].astype(F32)
            for i in range(3):
                total = total + r2[i, j].astype(F32)
            out[j] = scale * total

    def sides(h):
        for j in (2 * h, 2 * h + 1):
            f = nn(r.v_spread[...], r.seen[j].reshape(MB, 2 * T)).astype(BF)
            r.lhs_left[j] = f.reshape(2, 256, 2 * T)
            f = nt(r.v_spread[...], r.hidden[j]).astype(BF)
            r.lhs_dright[j] = f.reshape(2, 256, T)

    def dleft_half(q, c):
        rows = [r.v_g[:, (2 * q + i) * DB : (2 * q + i + 1) * DB] for i in range(2)]
        return nn(r.lhs_dleft[q, c], jnp.concatenate(rows, axis=0))

    def right_half(j, c):
        both = [nt(r.lhs_right[c], rhs[...]) for rhs in (r.rhs_gright, r.rhs_uright)]
        both = [part.reshape(16, 1, 8, 896) for part in both]
        return jnp.concatenate(both, axis=1).reshape(256, 896)

    def token_part(h, k):
        part = tn(r.back[k, :, :T], r.turned_g[k, h])
        return part + tn(r.back[k, :, T:], r.turned_u[k, h])

    def right(h):
        def keep(ys, moved):
            r.back32[:, pl.ds(ys, 1)] = moved.reshape(KB, 1, 56, 2 * T)

        pairs("d%d" % h, from_d[h], r.v_back, keep)
        for k in range(KB):
            back = r.back32[k].reshape(224, 2 * T).astype(BF)
            r.back[k] = back
            r.rhs_gright[k * 224 : (k + 1) * 224, k * T : (k + 1) * T] = back[:, :T]
            r.rhs_uright[k * 224 : (k + 1) * 224, k * T : (k + 1) * T] = back[:, T:]
        start_core("right%d" % h, (0,), right_half)

    def left(h):
        sides(h)
        parts = [
            ("left%d" % h, (0, 1), lambda i, c: nn(r.lhs_left[2 * h + i, c], r.rhs_left[2 * h + i])),
            ("dright%d" % h, (0, 1), lambda i, c: nt(r.lhs_dright[2 * h + i, c], r.dback[2 * h + i])),
        ]
        for part in parts:
            start_core(*part)
        for part in parts:
            start_x(*part)

    sent(from_a[0])
    from_c = exchange("c")
    forward(0)
    sent(from_c)
    from_a.append(exchange("a1"))
    arrived(from_c)
    unswap(lambda s: r.r_c[s], r.dback32, r.dback)
    backward(0)
    left(0)
    sent(from_a[1])
    from_d = [exchange("d0")]
    forward(1)
    backward(1)
    left(1)
    sent(from_d[0])
    from_d.append(exchange("d1"))

    right(0)
    for k in range(KB):
        r.tok[:, k * DB : (k + 1) * DB] = token_part(0, k)
    start_x("right0", (0,), right_half)
    from_b = [exchange("b0"), exchange("b1")]

    for name in ("left0", "dright0", "left1", "dright1"):
        start_pair(name, 2)

    right(1)
    start_far("left0", 2)
    start_far("dright0", 2)
    start_x("right1", (0,), right_half)
    start_far("left1", 2)
    start_far("dright1", 2)
    start_z("right0", 1)

    for copies in from_b:
        arrived(copies)
    unswap(lambda s: jnp.concatenate([r.r_b0[s], r.r_b1[s]], axis=0), r.dseen32, r.dseen)
    for j in range(KB):
        f = nn(r.v_twin[j % 2], r.dseen[j]).astype(BF)
        r.lhs_dleft[j // 2, :, :, (j % 2) * T : (j % 2 + 1) * T] = f.reshape(2, 256, T)
    start_core("dleft", (0, 1), dleft_half)
    for k in range(KB):
        columns = slice(k * DB, (k + 1) * DB)
        r.gtok[:, columns] = (r.tok[:, columns] + token_part(1, k)).astype(BF)
    start_x("dleft", (0, 1), dleft_half)
    start_z("right1", 1)
    for j in range(KB):
        r.mixed[:, j * DB : (j + 1) * DB] = tn(r.dseen[j], r.dl[j]).astype(BF)
    start_z("dleft", 2)
    finish("right0", 1)
    for name in PAIRED:
        finish_far(name, 2)
    finish("right1", 1)
    finish("dleft", 2)
    for copy in pending:
        copy.wait_send()


def unpack(names, *refs):
    r = types.SimpleNamespace(**dict(zip(names, refs)))
    copies = [
        pltpu.make_async_copy(r.mixed_in, r.mixed, r.sem.at[0]),
        pltpu.make_async_copy(r.gtok_in, r.gtok, r.sem.at[1]),
    ]
    for i, name in enumerate(UNPACKED):
        copies.append(pltpu.make_async_copy(vars(r)["h_" + name], vars(r)[name], r.sem.at[2 + i]))
    for copy in copies:
        copy.start()
    for copy in copies[2:]:
        copy.wait()
    total = None
    for h, source in enumerate((r.right0, r.right1)):
        rows = source[0]
        parts = [rows[:, :256]] + [pltpu.roll(rows, 896 - 224 * k, 1)[:, :256] for k in (1, 2, 3)]
        part = lax.dot_general(
            jnp.concatenate(parts, axis=0),
            r.columns[h],
            (((1,), (0,)), ((), ())),
            precision=lax.Precision.HIGHEST,
            preferred_element_type=F32,
        )
        total = part if total is None else total + part
    for k in range(KB):
        r.gr[:, k, :] = total[k * 16 : k * 16 + 8]
        r.ur[:, k, :] = total[k * 16 + 8 : k * 16 + 16]
    for j in range(KB):
        rows = (r.left0, r.left1)[j // 2][j % 2]
        r.gl[:, j, :] = rows[:MS, :MB]
        r.ul[:, j, :] = rows[:MS, MB:]
        r.dr[:, j, :] = (r.dright0, r.dright1)[j // 2][j % 2][:MS]
        r.dl[:, j, :] = r.dleft[j // 2][(j % 2) * 8 : (j % 2 + 1) * 8]
    for copy in copies[:2]:
        copy.wait()


def local(tokens, gate_right, gate_left, upward_right, upward_left, down_right, down_left, cotangent):
    scale = float(tokens.shape[0] * lax.axis_size("dp")) ** (-0.5)
    given = {
        "x": tokens,
        "g": cotangent,
        "wgr": jnp.transpose(gate_right, (1, 2, 0)),
        "wur": jnp.transpose(upward_right, (1, 2, 0)),
        "wdl": down_left,
        "wgl": gate_left,
        "wul": upward_left,
        "wdr": down_right,
    }
    given.update({name: jnp.asarray(value) for name, value in permutations().items()})
    scratch = scratch_list()
    names = ["h_" + name for name in INPUTS] + list(OUTS) + [name for name, _ in scratch]
    shapes = [jax.ShapeDtypeStruct((T, KB * DB), BF)] * 2
    shapes += [jax.ShapeDtypeStruct((count, 16, lanes), F32) for _, count, lanes in GROUPS]

    def body(*refs):
        kernel(scale, names, *refs)

    results = pl.pallas_call(
        body,
        out_shape=shapes,
        in_specs=[pl.BlockSpec(memory_space=pl.ANY)] * len(INPUTS),
        out_specs=[pl.BlockSpec(memory_space=pltpu.VMEM)] * len(OUTS),
        scratch_shapes=[shape for _, shape in scratch],
        compiler_params=pltpu.CompilerParams(
            collective_id=0, has_side_effects=True, vmem_limit_bytes=VMEM_LIMIT
        ),
        name="monarch",
    )(*[given[name] for name in INPUTS])

    last = [
        ((T, KB * DB), BF),
        ((T, KB * DB), BF),
        ((8, KB, MB), F32),
        ((MS, KB, MB), F32),
        ((8, KB, MB), F32),
        ((MS, KB, MB), F32),
        ((MS, KB, DB), F32),
        ((8, KB, DB), F32),
    ]
    anywhere, vmem = pl.BlockSpec(memory_space=pl.ANY), pl.BlockSpec(memory_space=pltpu.VMEM)
    parts = list(results[2:]) + [jnp.asarray(untangle())]
    names = ["mixed_in", "gtok_in"] + ["h_" + name for name in UNPACKED]
    names += ["mixed", "gtok", "gr", "gl", "ur", "ul", "dr", "dl"] + list(UNPACKED) + ["sem"]
    return pl.pallas_call(
        lambda *refs: unpack(names, *refs),
        out_shape=[jax.ShapeDtypeStruct(*entry) for entry in last],
        in_specs=[anywhere] * (2 + len(parts)),
        out_specs=[vmem] * 8,
        scratch_shapes=[pltpu.VMEM(part.shape, F32) for part in parts]
        + [pltpu.SemaphoreType.DMA((2 + len(parts),))],
        compiler_params=pltpu.CompilerParams(vmem_limit_bytes=VMEM_LIMIT),
        name="unpack",
    )(*results[:2], *parts)


def solution(mesh):
    weight = P(None, "blk", None)
    grad = P("dp", "blk", None)
    return jax.shard_map(
        local,
        mesh=mesh,
        in_specs=(P("dp", "blk"),) + (weight,) * 6 + (P("dp", "blk"),),
        out_specs=(P("dp", "blk"),) * 2 + (grad,) * 6,
        check_vma=False,
    )
```

```python
import types

import jax
import jax.numpy as jnp
import numpy as np
from jax import lax
from jax.experimental import pallas as pl
from jax.experimental.pallas import tpu as pltpu
from jax.sharding import PartitionSpec as P

BF = jnp.bfloat16
F32 = jnp.float32
MESH = pl.DeviceIdType.MESH

NB = 32
KB = 4
DB = 256
MB = 448
MS = 14
T = 128
VMEM_LIMIT = 60 * 1024 * 1024
X, Z, Y = 4, 4, 4
OFFS = ((0, 1), (1, 1), (3, 1), (2, 1), (1, 0), (3, 0), (2, 0))


def permutations():
    take = np.zeros((224, 224), np.float32)
    meet = np.zeros((224, 224), np.float32)
    back = np.zeros((224, 224), np.float32)
    for k in range(4):
        for h in range(2):
            for j in range(2):
                for r in range(MS):
                    take[((h * 4 + k) * 2 + j) * MS + r, ((k * 2 + h) * 2 + j) * MS + r] = 1.0
                    meet[((j * 2 + h) * 4 + k) * MS + r, ((h * 4 + k) * 2 + j) * MS + r] = 1.0
                    back[((k * 2 + h) * 2 + j) * MS + r, ((h * 2 + j) * 4 + k) * MS + r] = 1.0
    turn = np.zeros((448, 448), np.float32)
    for p in range(8):
        for h in range(2):
            for i in range(2 * MS):
                turn[h * 224 + p * 28 + i, p * 56 + h * 28 + i] = 1.0
    spread = np.zeros((2, 256, 448), np.float32)
    order = np.zeros((2, 128, 256), np.float32)
    twin = np.zeros((2, 2, 256, 256), np.float32)
    for c in range(2):
        for x in range(X):
            for z in range(Z):
                d = z * 8 + x * 2 + c
                for i in range(MS):
                    spread[c, (x * 4 + z) * 16 + i, d * MS + i] = 1.0
                for i in range(8):
                    order[c, (x * 4 + z) * 8 + i, d * 8 + i] = 1.0
                    for q in range(2):
                        twin[q, c, (x * 4 + z) * 16 + q * 8 + i, d * 8 + i] = 1.0
    out = {
        "take": take,
        "meet": meet,
        "back": back,
        "turn": turn,
        "spread": spread.reshape(512, 448),
        "order": order.reshape(256, 256),
        "twin": twin.reshape(2, 512, 256),
    }
    return {name: np.asarray(value, jnp.bfloat16) for name, value in out.items()}


def untangle():
    out = np.zeros((2, 256, 448), np.float32)
    for h in range(2):
        for p in range(8):
            for i in range(2 * MS):
                out[h, p * 28 + i, p * 56 + h * 28 + i] = 1.0
    return out


def nn(a, b):
    return lax.dot_general(a, b, (((1,), (0,)), ((), ())), preferred_element_type=F32)


def nt(a, b):
    return lax.dot_general(a, b, (((1,), (1,)), ((), ())), preferred_element_type=F32)


def tn(a, b):
    return lax.dot_general(a, b, (((0,), (0,)), ((), ())), preferred_element_type=F32)


INPUTS = (
    "x",
    "wgr",
    "wur",
    "take",
    "wdl",
    "g",
    "wgl",
    "wul",
    "wdr",
    "meet",
    "order",
    "turn",
    "back",
    "spread",
    "twin",
)
FIRST = 4
SHAPES = {
    "x": (T, KB * DB),
    "g": (T, KB * DB),
    "wgr": (KB, MB, DB),
    "wur": (KB, MB, DB),
    "wdl": (DB, KB, DB),
    "wgl": (MB, KB, MB),
    "wul": (MB, KB, MB),
    "wdr": (MB, KB, DB),
    "take": (224, 224),
    "meet": (224, 224),
    "back": (224, 224),
    "turn": (448, 448),
    "spread": (512, 448),
    "order": (256, 256),
    "twin": (2, 512, 256),
}
GROUPS = (
    ("left0", 2, 896),
    ("left1", 2, 896),
    ("dright0", 2, 256),
    ("dright1", 2, 256),
    ("dleft", 2, 256),
    ("right0", 1, 896),
    ("right1", 1, 896),
)
PAIRED = ("left0", "left1", "dright0", "dright1")
UNPACKED = PAIRED + ("dleft", "right0", "right1", "columns")
OUTS = ("mixed", "gtok") + tuple("o_" + name for name, _, _ in GROUPS)
SLABS = (
    ("a0", (112, 256)),
    ("a1", (112, 256)),
    ("d0", (112, 256)),
    ("d1", (112, 256)),
    ("b0", (64, T)),
    ("b1", (64, T)),
    ("c", (128, T)),
)


def scratch_list():
    out = []

    def add(name, shape, dtype=BF):
        out.append((name, pltpu.VMEM(shape, dtype)))

    for name in INPUTS:
        add("v_" + name, SHAPES[name])
    out.append(("in_sem", pltpu.SemaphoreType.DMA((len(INPUTS),))))
    for name, slab in SLABS:
        add("s_" + name, (8,) + slab)
        add("r_" + name, (8,) + slab)
        out.append(("ss_" + name, pltpu.SemaphoreType.DMA((7,))))
        out.append(("rs_" + name, pltpu.SemaphoreType.DMA((7,))))
    add("gl", (KB, MB, MB))
    add("ul", (KB, MB, MB))
    add("dr", (KB, DB, MB))
    add("dl", (KB, DB, DB))
    add("turned_g", (KB, 2, 224, DB))
    add("turned_u", (KB, 2, 224, DB))
    add("flow", (KB, MB, 2 * T), F32)
    add("seen", (KB, Y, 112, 2 * T))
    add("back32", (KB, Y, 56, 2 * T), F32)
    add("back", (KB, 224, 2 * T))
    add("act", (KB, T, MB), F32)
    add("slope", (KB, T, MB), F32)
    add("hidden", (KB, T, MB))
    add("dback32", (KB, 8, 4, 8, T), F32)
    add("dseen32", (KB, 8, 4, 8, T), F32)
    add("dback", (KB, DB, T))
    add("dseen", (KB, DB, T))
    add("lhs_left", (KB, 2, 256, 256))
    add("rhs_left", (KB, 256, 896))
    add("lhs_dright", (KB, 2, 256, T))
    add("lhs_dleft", (2, 2, 256, 256))
    add("lhs_right", (2, 128, 512))
    add("rhs_gright", (896, 512))
    add("rhs_uright", (896, 512))
    add("tok", (T, KB * DB), F32)
    add("w_mixed", (T, KB * DB))
    add("w_gtok", (T, KB * DB))
    out.append(("out_sem", pltpu.SemaphoreType.DMA((2,))))
    for name, count, lanes in GROUPS:
        add("s0_" + name, (count, 256, lanes))
        add("r0_" + name, (count, 256, lanes))
        add("s1_" + name, (count, X, 64, lanes))
        add("r1_" + name, (count, 3, 64, lanes))
        if name in PAIRED:
            add("s2_" + name, (count, 2, 2, 16, lanes))
            add("r2_" + name, (count, 2, 16, lanes))
            add("s3_" + name, (count, 2, 16, lanes))
            add("r3_" + name, (count, 16, lanes))
        else:
            add("s2_" + name, (count, Z, 16, lanes))
            add("r2_" + name, (3, count, 16, lanes))
        for kind in ("ss0_", "rs0_"):
            out.append((kind + name, pltpu.SemaphoreType.DMA((count,))))
        for kind in ("ss1_", "rs1_"):
            out.append((kind + name, pltpu.SemaphoreType.DMA((count * 3,))))
        for kind in ("ss2_", "rs2_"):
            out.append((kind + name, pltpu.SemaphoreType.DMA((3,))))
    return out


def loop(count, body):
    lax.fori_loop(0, count, lambda i, _: (body(i), 0)[1], 0)


def kernel(scale, names, *refs):
    r = types.SimpleNamespace(**dict(zip(names, refs)))
    v = vars(r)
    dp = lax.axis_index("dp")
    blk = lax.axis_index("blk")
    core, x, z = dp % 2, (dp // 2) % X, dp // 8
    y, zh = blk // 2, blk % 2
    pending = []

    loads = {}
    for i, name in enumerate(INPUTS):
        loads[name] = pltpu.make_async_copy(v["h_" + name], v["v_" + name], r.in_sem.at[i])

    def load(*which):
        for name in which:
            loads[name].start()

    load(*INPUTS[:FIRST])

    def need(*which):
        for name in which:
            loads[name].wait()

    def blk_peer(dy, dz):
        return ((y + dy) % Y) * 2 + (zh + dz) % 2

    def dp_id(z_, x_, c_):
        return (z_ * 8 + x_ * 2 + c_, blk)

    core_id = dp_id(z, x, 1 - core)
    x_ids = [dp_id(z, (x + d) % X, core) for d in (1, 2, 3)]
    z_ids = [dp_id((z + d) % Z, x, core) for d in (1, 2, 3)]
    everyone = [(dp, blk_peer(dy, dz)) for dy, dz in OFFS] + [core_id] + x_ids + z_ids

    barrier = pltpu.get_barrier_semaphore()
    for who in everyone:
        pl.semaphore_signal(barrier, inc=1, device_id=who, device_id_type=MESH)

    def remote(src, dst, ss, rs, who):
        copy = pltpu.make_async_remote_copy(
            src_ref=src, dst_ref=dst, send_sem=ss, recv_sem=rs, device_id=who, device_id_type=MESH
        )
        copy.start()
        pending.append(copy)
        return copy

    def exchange(name):
        s, d, ss, rs = (v[k + name] for k in ("s_", "r_", "ss_", "rs_"))
        out = {}
        for i, (dy, dz) in enumerate(OFFS):
            p = blk_peer(dy, dz)
            out[dy, dz] = remote(s.at[p], d.at[blk], ss.at[i], rs.at[i], (dp, p))
        d[blk] = s[blk]
        return out

    def pairs(name, copies, matrix, use):
        for dy in range(4):
            for dz in range(2):
                if (dy, dz) != (0, 0):
                    copies[dy, dz].wait_recv()
            ys = (y - dy + Y) % Y
            two = v["r_" + name][pl.ds(ys * 2, 2)].reshape(224, 2 * T)
            use(ys, nn(matrix[...], two))

    def unswap(source, wide, out):
        def one(s):
            got = source(s).astype(F32).reshape(4, 4, 8, T)
            for a in range(4):
                for b in range(4):
                    wide[b, s, a] = got[a, b]

        loop(8, one)
        for b in range(KB):
            out[b] = wide[b].reshape(DB, T).astype(BF)

    def arrived(copies):
        for copy in copies.values():
            copy.wait_recv()

    def sent(copies):
        for copy in copies.values():
            copy.wait_send()
        gone = {id(copy) for copy in copies.values()}
        pending[:] = [copy for copy in pending if id(copy) not in gone]

    need(*INPUTS[:FIRST])
    load(*INPUTS[FIRST:])
    for k in range(KB):
        xk = r.v_x[:, k * DB : (k + 1) * DB]
        r.flow[k, :, :T] = nt(r.v_wgr[k], xk)
        r.flow[k, :, T:] = nt(r.v_wur[k], xk)
    for p in range(8):
        rows = r.flow[:, p * 56 : (p + 1) * 56, :].reshape(224, 2 * T).astype(BF)
        taken = nn(r.v_take[...], rows).astype(BF)
        r.s_a0[p] = taken[:112]
        r.s_a1[p] = taken[112:]
    pl.semaphore_wait(barrier, len(everyone))
    from_a = [exchange("a0")]

    need("wdl", "g")
    r.dl[...] = jnp.swapaxes(r.v_wdl[...], 0, 1)
    for j in range(KB):
        f = nt(r.dl[j], r.v_g[:, j * DB : (j + 1) * DB]).astype(BF)
        r.s_c[:, j * 32 : (j + 1) * 32, :] = f.reshape(8, 32, T)

    need("wgl", "wul", "wdr", "meet", "order", "turn", "back", "spread", "twin")
    r.gl[...] = jnp.swapaxes(r.v_wgl[...], 0, 1)
    r.ul[...] = jnp.swapaxes(r.v_wul[...], 0, 1)
    eye = lax.broadcasted_iota(jnp.int32, (DB, DB), 0) == lax.broadcasted_iota(jnp.int32, (DB, DB), 1)
    eye = eye.astype(F32).astype(BF)
    swapped = jnp.swapaxes(r.v_wdr[...], 0, 1)
    for k in range(KB):
        r.dr[k] = nt(eye, swapped[k]).astype(BF)
    r.rhs_gright[...] = jnp.zeros_like(r.rhs_gright)
    r.rhs_uright[...] = jnp.zeros_like(r.rhs_uright)
    for k in range(KB):
        f = nt(r.v_order[...], r.v_x[:, k * DB : (k + 1) * DB]).astype(BF)
        r.lhs_right[:, :, k * T : (k + 1) * T] = f.reshape(2, 128, T)

    def turned(k):
        r.turned_g[k] = nn(r.v_turn[...], r.v_wgr[k]).astype(BF).reshape(2, 224, DB)
        r.turned_u[k] = nn(r.v_turn[...], r.v_wur[k]).astype(BF).reshape(2, 224, DB)

    loop(KB, turned)

    def forward(h):
        def keep(ys, moved):
            r.seen[2 * h : 2 * h + 2, pl.ds(ys, 1)] = moved.astype(BF).reshape(2, 1, 112, 2 * T)

        pairs("a%d" % h, from_a[h], r.v_meet, keep)
        for i in range(2):
            j = 2 * h + i
            seen = r.seen[j].reshape(MB, 2 * T)
            pre = tn(seen[:, :T], r.gl[j])
            up = tn(seen[:, T:], r.ul[j])
            sig = jax.nn.sigmoid(pre)
            act = pre * sig
            hidden = (act * up).astype(BF)
            r.act[j] = act
            r.slope[j] = up * sig * (1.0 + pre * (1.0 - sig))
            r.hidden[j] = hidden
            f = nt(r.dr[j], hidden).astype(BF)
            v["s_b%d" % h][:, i * 32 : (i + 1) * 32, :] = f.reshape(8, 32, T)

    def backward(h):
        for i in range(2):
            j = 2 * h + i
            hf = tn(r.dback[j], r.dr[j])
            gg = (hf * r.slope[j]).astype(BF)
            ug = (hf * r.act[j]).astype(BF)
            r.flow[i, :, :T] = nt(r.gl[j], gg)
            r.flow[i, :, T:] = nt(r.ul[j], ug)
            r.rhs_left[j, :T, :] = jnp.concatenate([gg, jnp.zeros((T, MB), BF)], axis=1)
            r.rhs_left[j, T:, :] = jnp.concatenate([jnp.zeros((T, MB), BF), ug], axis=1)
        for p in range(8):
            rows = r.flow[:2, p * 56 : (p + 1) * 56, :].reshape(112, 2 * T)
            v["s_d%d" % h][p] = rows.astype(BF)

    moves = {}

    def start_core(name, which, half):
        s0, r0, ss, rs = (v[k + name] for k in ("s0_", "r0_", "ss0_", "rs0_"))
        for j in which:
            s0[j] = half(j, 1 - core).astype(BF)
            moves[name, 0, j] = remote(s0.at[j], r0.at[j], ss.at[j], rs.at[j], core_id)

    def start_x(name, which, half):
        r0, s1, r1, ss, rs = (v[k + name] for k in ("r0_", "s1_", "r1_", "ss1_", "rs1_"))
        for j in which:
            own = half(j, core)
            moves[name, 0, j].wait_recv()
            s1[j] = (own + r0[j].astype(F32)).astype(BF).reshape(s1.shape[1:])
            for i in (0, 2, 1):
                moves[name, 1, j, i] = remote(
                    s1.at[j, (x + i + 1) % X],
                    r1.at[j, i],
                    ss.at[j * 3 + i],
                    rs.at[j * 3 + i],
                    x_ids[i],
                )

    def start_z(name, count):
        s1, r1, s2, r2, ss, rs = (
            v[k + name] for k in ("s1_", "r1_", "s2_", "r2_", "ss2_", "rs2_")
        )
        for j in range(count):
            for i in range(3):
                moves[name, 1, j, i].wait_recv()
            total = s1[j, x].astype(F32)
            for i in range(3):
                total = total + r1[j, i].astype(F32)
            s2[j] = total.astype(BF).reshape(s2.shape[1:])
        for i in range(3):
            moves[name, 2, i] = remote(
                s2.at[:, (z + i + 1) % Z], r2.at[i], ss.at[i], rs.at[i], z_ids[i]
            )

    def start_pair(name, count):
        s1, r1, s2, r2, ss, rs = (
            v[k + name] for k in ("s1_", "r1_", "s2_", "r2_", "ss2_", "rs2_")
        )
        for j in range(count):
            for i in range(3):
                moves[name, 1, j, i].wait_recv()
            total = s1[j, x].astype(F32)
            for i in range(3):
                total = total + r1[j, i].astype(F32)
            s2[j] = total.astype(BF).reshape(s2.shape[1:])
        near = z + 1 - 2 * (z % 2)
        moves[name, 2] = remote(
            s2.at[:, :, 1 - z % 2], r2, ss.at[0], rs.at[0], dp_id(near, x, core)
        )

    def start_far(name, count):
        s2, r2, s3, r3, ss, rs = (
            v[k + name] for k in ("s2_", "r2_", "s3_", "r3_", "ss2_", "rs2_")
        )
        moves[name, 2].wait_recv()
        for j in range(count):
            for i in range(2):
                s3[j, i] = (s2[j, i, z % 2].astype(F32) + r2[j, i].astype(F32)).astype(BF)
        moves[name, 3] = remote(
            s3.at[:, 1 - z // 2], r3, ss.at[1], rs.at[1], dp_id((z + 2) % Z, x, core)
        )

    def finish_far(name, count):
        s3, r3, out = v["s3_" + name], v["r3_" + name], v["o_" + name]
        moves[name, 3].wait_recv()
        for j in range(count):
            out[j] = scale * (s3[j, z // 2].astype(F32) + r3[j].astype(F32))

    def finish(name, count):
        s2, r2, out = v["s2_" + name], v["r2_" + name], v["o_" + name]
        for i in range(3):
            moves[name, 2, i].wait_recv()
        for j in range(count):
            total = s2[j, z].astype(F32)
            for i in range(3):
                total = total + r2[i, j].astype(F32)
            out[j] = scale * total

    def sides(h):
        for j in (2 * h, 2 * h + 1):
            f = nn(r.v_spread[...], r.seen[j].reshape(MB, 2 * T)).astype(BF)
            r.lhs_left[j] = f.reshape(2, 256, 2 * T)
            f = nt(r.v_spread[...], r.hidden[j]).astype(BF)
            r.lhs_dright[j] = f.reshape(2, 256, T)

    def dleft_half(q, c):
        rows = [r.v_g[:, (2 * q + i) * DB : (2 * q + i + 1) * DB] for i in range(2)]
        return nn(r.lhs_dleft[q, c], jnp.concatenate(rows, axis=0))

    def right_half(j, c):
        both = [nt(r.lhs_right[c], rhs[...]) for rhs in (r.rhs_gright, r.rhs_uright)]
        both = [part.reshape(16, 1, 8, 896) for part in both]
        return jnp.concatenate(both, axis=1).reshape(256, 896)

    def token_part(h, k):
        part = tn(r.back[k, :, :T], r.turned_g[k, h])
        return part + tn(r.back[k, :, T:], r.turned_u[k, h])

    def right(h):
        def keep(ys, moved):
            r.back32[:, pl.ds(ys, 1)] = moved.reshape(KB, 1, 56, 2 * T)

        pairs("d%d" % h, from_d[h], r.v_back, keep)
        for k in range(KB):
            back = r.back32[k].reshape(224, 2 * T).astype(BF)
            r.back[k] = back
            r.rhs_gright[k * 224 : (k + 1) * 224, k * T : (k + 1) * T] = back[:, :T]
            r.rhs_uright[k * 224 : (k + 1) * 224, k * T : (k + 1) * T] = back[:, T:]
        start_core("right%d" % h, (0,), right_half)

    def left(h):
        sides(h)
        parts = [
            ("left%d" % h, (0, 1), lambda i, c: nn(r.lhs_left[2 * h + i, c], r.rhs_left[2 * h + i])),
            ("dright%d" % h, (0, 1), lambda i, c: nt(r.lhs_dright[2 * h + i, c], r.dback[2 * h + i])),
        ]
        for part in parts:
            start_core(*part)
        for part in parts:
            start_x(*part)

    sent(from_a[0])
    from_c = exchange("c")
    forward(0)
    sent(from_c)
    from_a.append(exchange("a1"))
    arrived(from_c)
    unswap(lambda s: r.r_c[s], r.dback32, r.dback)
    backward(0)
    left(0)
    sent(from_a[1])
    from_d = [exchange("d0")]
    forward(1)
    backward(1)
    left(1)
    sent(from_d[0])
    from_d.append(exchange("d1"))

    right(0)
    for k in range(KB):
        r.tok[:, k * DB : (k + 1) * DB] = token_part(0, k)
    start_x("right0", (0,), right_half)
    from_b = [exchange("b0"), exchange("b1")]

    for name in ("left0", "dright0", "left1", "dright1"):
        start_pair(name, 2)

    right(1)
    start_far("left0", 2)
    start_far("dright0", 2)
    start_x("right1", (0,), right_half)
    start_far("left1", 2)
    start_far("dright1", 2)
    start_z("right0", 1)

    for copies in from_b:
        arrived(copies)
    unswap(lambda s: jnp.concatenate([r.r_b0[s], r.r_b1[s]], axis=0), r.dseen32, r.dseen)
    for j in range(KB):
        f = nn(r.v_twin[j % 2], r.dseen[j]).astype(BF)
        r.lhs_dleft[j // 2, :, :, (j % 2) * T : (j % 2 + 1) * T] = f.reshape(2, 256, T)
    start_core("dleft", (0, 1), dleft_half)
    for k in range(KB):
        columns = slice(k * DB, (k + 1) * DB)
        r.w_gtok[:, columns] = (r.tok[:, columns] + token_part(1, k)).astype(BF)
    out_gtok = pltpu.make_async_copy(r.w_gtok, r.gtok, r.out_sem.at[0])
    out_gtok.start()
    start_x("dleft", (0, 1), dleft_half)
    start_z("right1", 1)
    for j in range(KB):
        r.w_mixed[:, j * DB : (j + 1) * DB] = tn(r.dseen[j], r.dl[j]).astype(BF)
    out_mixed = pltpu.make_async_copy(r.w_mixed, r.mixed, r.out_sem.at[1])
    out_mixed.start()
    start_z("dleft", 2)
    finish("right0", 1)
    for name in PAIRED:
        finish_far(name, 2)
    finish("right1", 1)
    finish("dleft", 2)
    out_gtok.wait()
    out_mixed.wait()
    for copy in pending:
        copy.wait_send()


def unpack(names, *refs):
    r = types.SimpleNamespace(**dict(zip(names, refs)))
    copies = [
        pltpu.make_async_copy(r.mixed_in, r.mixed_held, r.sem.at[0]),
        pltpu.make_async_copy(r.gtok_in, r.gtok_held, r.sem.at[1]),
    ]
    for i, name in enumerate(UNPACKED):
        copies.append(pltpu.make_async_copy(vars(r)["h_" + name], vars(r)[name], r.sem.at[2 + i]))
    for copy in copies:
        copy.start()
    for copy in copies:
        copy.wait()
    onward = [
        pltpu.make_async_copy(r.mixed_held, r.mixed, r.out_sem.at[0]),
        pltpu.make_async_copy(r.gtok_held, r.gtok, r.out_sem.at[1]),
    ]
    for copy in onward:
        copy.start()
    total = None
    for h, source in enumerate((r.right0, r.right1)):
        rows = source[0]
        parts = [rows[:, :256]] + [pltpu.roll(rows, 896 - 224 * k, 1)[:, :256] for k in (1, 2, 3)]
        part = lax.dot_general(
            jnp.concatenate(parts, axis=0),
            r.columns[h],
            (((1,), (0,)), ((), ())),
            precision=lax.Precision.HIGHEST,
            preferred_element_type=F32,
        )
        total = part if total is None else total + part
    for k in range(KB):
        r.gr[:, k, :] = total[k * 16 : k * 16 + 8]
        r.ur[:, k, :] = total[k * 16 + 8 : k * 16 + 16]
    for j in range(KB):
        rows = (r.left0, r.left1)[j // 2][j % 2]
        r.gl[:, j, :] = rows[:MS, :MB]
        r.ul[:, j, :] = rows[:MS, MB:]
        r.dr[:, j, :] = (r.dright0, r.dright1)[j // 2][j % 2][:MS]
        r.dl[:, j, :] = r.dleft[j // 2][(j % 2) * 8 : (j % 2 + 1) * 8]
    for copy in onward:
        copy.wait()


def local(tokens, gate_right, gate_left, upward_right, upward_left, down_right, down_left, cotangent):
    scale = float(tokens.shape[0] * lax.axis_size("dp")) ** (-0.5)
    given = {
        "x": tokens,
        "g": cotangent,
        "wgr": jnp.transpose(gate_right, (1, 2, 0)),
        "wur": jnp.transpose(upward_right, (1, 2, 0)),
        "wdl": down_left,
        "wgl": gate_left,
        "wul": upward_left,
        "wdr": down_right,
    }
    given.update({name: jnp.asarray(value) for name, value in permutations().items()})
    scratch = scratch_list()
    names = ["h_" + name for name in INPUTS] + list(OUTS) + [name for name, _ in scratch]
    shapes = [jax.ShapeDtypeStruct((T, KB * DB), BF)] * 2
    shapes += [jax.ShapeDtypeStruct((count, 16, lanes), F32) for _, count, lanes in GROUPS]

    def body(*refs):
        kernel(scale, names, *refs)

    results = pl.pallas_call(
        body,
        out_shape=shapes,
        in_specs=[pl.BlockSpec(memory_space=pl.ANY)] * len(INPUTS),
        out_specs=[pl.BlockSpec(memory_space=pl.ANY)] * 2
        + [pl.BlockSpec(memory_space=pltpu.VMEM)] * (len(OUTS) - 2),
        scratch_shapes=[shape for _, shape in scratch],
        compiler_params=pltpu.CompilerParams(
            collective_id=0, has_side_effects=True, vmem_limit_bytes=VMEM_LIMIT
        ),
        name="monarch",
    )(*[given[name] for name in INPUTS])

    last = [
        ((T, KB * DB), BF),
        ((T, KB * DB), BF),
        ((8, KB, MB), F32),
        ((MS, KB, MB), F32),
        ((8, KB, MB), F32),
        ((MS, KB, MB), F32),
        ((MS, KB, DB), F32),
        ((8, KB, DB), F32),
    ]
    anywhere, vmem = pl.BlockSpec(memory_space=pl.ANY), pl.BlockSpec(memory_space=pltpu.VMEM)
    parts = list(results[2:]) + [jnp.asarray(untangle())]
    names = ["mixed_in", "gtok_in"] + ["h_" + name for name in UNPACKED]
    names += ["mixed", "gtok", "gr", "gl", "ur", "ul", "dr", "dl"] + list(UNPACKED)
    names += ["mixed_held", "gtok_held", "sem", "out_sem"]
    return pl.pallas_call(
        lambda *refs: unpack(names, *refs),
        out_shape=[jax.ShapeDtypeStruct(*entry) for entry in last],
        in_specs=[anywhere] * (2 + len(parts)),
        out_specs=[anywhere] * 2 + [vmem] * 6,
        scratch_shapes=[pltpu.VMEM(part.shape, F32) for part in parts]
        + [pltpu.VMEM((T, KB * DB), BF)] * 2
        + [pltpu.SemaphoreType.DMA((2 + len(parts),)), pltpu.SemaphoreType.DMA((2,))],
        compiler_params=pltpu.CompilerParams(vmem_limit_bytes=VMEM_LIMIT),
        name="unpack",
    )(*results[:2], *parts)


def solution(mesh):
    weight = P(None, "blk", None)
    grad = P("dp", "blk", None)
    return jax.shard_map(
        local,
        mesh=mesh,
        in_specs=(P("dp", "blk"),) + (weight,) * 6 + (P("dp", "blk"),),
        out_specs=(P("dp", "blk"),) * 2 + (grad,) * 6,
        check_vma=False,
    )
```

```python
import types

import jax
import jax.numpy as jnp
import numpy as np
from jax import lax
from jax.experimental import pallas as pl
from jax.experimental.pallas import tpu as pltpu
from jax.sharding import PartitionSpec as P

BF = jnp.bfloat16
F32 = jnp.float32
MESH = pl.DeviceIdType.MESH

NB = 32
KB = 4
DB = 256
MB = 448
MS = 14
T = 128
VMEM_LIMIT = 60 * 1024 * 1024
X, Z, Y = 4, 4, 4
OFFS = ((0, 1), (1, 1), (3, 1), (2, 1), (1, 0), (3, 0), (2, 0))


def permutations():
    take = np.zeros((224, 224), np.float32)
    meet = np.zeros((224, 224), np.float32)
    back = np.zeros((224, 224), np.float32)
    for k in range(4):
        for h in range(2):
            for j in range(2):
                for r in range(MS):
                    take[((h * 4 + k) * 2 + j) * MS + r, ((k * 2 + h) * 2 + j) * MS + r] = 1.0
                    meet[((j * 2 + h) * 4 + k) * MS + r, ((h * 4 + k) * 2 + j) * MS + r] = 1.0
                    back[((k * 2 + h) * 2 + j) * MS + r, ((h * 2 + j) * 4 + k) * MS + r] = 1.0
    turn = np.zeros((448, 448), np.float32)
    for p in range(8):
        for h in range(2):
            for i in range(2 * MS):
                turn[h * 224 + p * 28 + i, p * 56 + h * 28 + i] = 1.0
    spread = np.zeros((2, 256, 448), np.float32)
    order = np.zeros((2, 128, 256), np.float32)
    twin = np.zeros((2, 2, 256, 256), np.float32)
    for c in range(2):
        for x in range(X):
            for z in range(Z):
                d = z * 8 + x * 2 + c
                for i in range(MS):
                    spread[c, (x * 4 + z) * 16 + i, d * MS + i] = 1.0
                for i in range(8):
                    order[c, (x * 4 + z) * 8 + i, d * 8 + i] = 1.0
                    for q in range(2):
                        twin[q, c, (x * 4 + z) * 16 + q * 8 + i, d * 8 + i] = 1.0
    out = {
        "take": take,
        "meet": meet,
        "back": back,
        "turn": turn,
        "spread": spread.reshape(512, 448),
        "order": order.reshape(256, 256),
        "twin": twin.reshape(2, 512, 256),
    }
    return {name: np.asarray(value, jnp.bfloat16) for name, value in out.items()}


def untangle():
    out = np.zeros((2, 256, 448), np.float32)
    for h in range(2):
        for p in range(8):
            for i in range(2 * MS):
                out[h, p * 28 + i, p * 56 + h * 28 + i] = 1.0
    return out


def nn(a, b):
    return lax.dot_general(a, b, (((1,), (0,)), ((), ())), preferred_element_type=F32)


def nt(a, b):
    return lax.dot_general(a, b, (((1,), (1,)), ((), ())), preferred_element_type=F32)


def tn(a, b):
    return lax.dot_general(a, b, (((0,), (0,)), ((), ())), preferred_element_type=F32)


INPUTS = (
    "x",
    "wgr",
    "wur",
    "take",
    "wdl",
    "g",
    "wgl",
    "wul",
    "wdr",
    "meet",
    "order",
    "turn",
    "back",
    "spread",
    "twin",
)
FIRST = 4
SHAPES = {
    "x": (T, KB * DB),
    "g": (T, KB * DB),
    "wgr": (KB, MB, DB),
    "wur": (KB, MB, DB),
    "wdl": (DB, KB, DB),
    "wgl": (MB, KB, MB),
    "wul": (MB, KB, MB),
    "wdr": (MB, KB, DB),
    "take": (224, 224),
    "meet": (224, 224),
    "back": (224, 224),
    "turn": (448, 448),
    "spread": (512, 448),
    "order": (256, 256),
    "twin": (2, 512, 256),
}
GROUPS = (
    ("left0", 2, 896),
    ("left1", 2, 896),
    ("dright0", 2, 256),
    ("dright1", 2, 256),
    ("dleft", 2, 256),
    ("right0", 1, 896),
    ("right1", 1, 896),
)
PAIRED = ("left0", "left1", "dright0", "dright1")
UNPACKED = PAIRED + ("dleft", "right0", "right1", "columns")
OUTS = ("mixed", "gtok") + tuple("o_" + name for name, _, _ in GROUPS)
SLABS = (
    ("a0", (112, 256)),
    ("a1", (112, 256)),
    ("d0", (112, 256)),
    ("d1", (112, 256)),
    ("b0", (64, T)),
    ("b1", (64, T)),
    ("c", (128, T)),
)


def scratch_list():
    out = []

    def add(name, shape, dtype=BF):
        out.append((name, pltpu.VMEM(shape, dtype)))

    for name in INPUTS:
        add("v_" + name, SHAPES[name])
    out.append(("in_sem", pltpu.SemaphoreType.DMA((len(INPUTS),))))
    for name, slab in SLABS:
        add("s_" + name, (8,) + slab)
        add("r_" + name, (8,) + slab)
        out.append(("ss_" + name, pltpu.SemaphoreType.DMA((7,))))
        out.append(("rs_" + name, pltpu.SemaphoreType.DMA((7,))))
    add("gl", (KB, MB, MB))
    add("ul", (KB, MB, MB))
    add("dr", (KB, DB, MB))
    add("dl", (KB, DB, DB))
    add("turned_g", (KB, 2, 224, DB))
    add("turned_u", (KB, 2, 224, DB))
    add("flow", (KB, MB, 2 * T), F32)
    add("seen", (KB, Y, 112, 2 * T))
    add("back32", (KB, Y, 56, 2 * T), F32)
    add("back", (KB, 224, 2 * T))
    add("act", (KB, T, MB), F32)
    add("slope", (KB, T, MB), F32)
    add("hidden", (KB, T, MB))
    add("dback32", (KB, 8, 4, 8, T), F32)
    add("dseen32", (KB, 8, 4, 8, T), F32)
    add("dback", (KB, DB, T))
    add("dseen", (KB, DB, T))
    add("lhs_left", (KB, 2, 256, 256))
    add("rhs_left", (KB, 256, 896))
    add("lhs_dright", (KB, 2, 256, T))
    add("lhs_dleft", (2, 2, 256, 256))
    add("lhs_right", (2, 128, 512))
    add("rhs_gright", (896, 512))
    add("rhs_uright", (896, 512))
    add("tok", (T, KB * DB), F32)
    add("w_mixed", (T, KB * DB))
    add("w_gtok", (T, KB * DB))
    out.append(("out_sem", pltpu.SemaphoreType.DMA((2,))))
    for name, count, lanes in GROUPS:
        add("s0_" + name, (count, 256, lanes))
        add("r0_" + name, (count, 256, lanes))
        add("s1_" + name, (count, X, 64, lanes))
        add("r1_" + name, (count, 3, 64, lanes))
        if name in PAIRED:
            add("s2_" + name, (count, 2, 2, 16, lanes))
            add("r2_" + name, (count, 2, 16, lanes))
            add("s3_" + name, (count, 2, 16, lanes))
            add("r3_" + name, (count, 16, lanes))
        else:
            add("s2_" + name, (count, Z, 16, lanes))
            add("r2_" + name, (3, count, 16, lanes))
        for kind in ("ss0_", "rs0_"):
            out.append((kind + name, pltpu.SemaphoreType.DMA((count,))))
        for kind in ("ss1_", "rs1_"):
            out.append((kind + name, pltpu.SemaphoreType.DMA((count * 3,))))
        for kind in ("ss2_", "rs2_"):
            out.append((kind + name, pltpu.SemaphoreType.DMA((3,))))
    return out


def loop(count, body):
    lax.fori_loop(0, count, lambda i, _: (body(i), 0)[1], 0)


def kernel(scale, names, *refs):
    r = types.SimpleNamespace(**dict(zip(names, refs)))
    v = vars(r)
    dp = lax.axis_index("dp")
    blk = lax.axis_index("blk")
    core, x, z = dp % 2, (dp // 2) % X, dp // 8
    y, zh = blk // 2, blk % 2
    pending = []

    loads = {}
    for i, name in enumerate(INPUTS):
        loads[name] = pltpu.make_async_copy(v["h_" + name], v["v_" + name], r.in_sem.at[i])

    def load(*which):
        for name in which:
            loads[name].start()

    load(*INPUTS[:FIRST])

    def need(*which):
        for name in which:
            loads[name].wait()

    def blk_peer(dy, dz):
        return ((y + dy) % Y) * 2 + (zh + dz) % 2

    def dp_id(z_, x_, c_):
        return (z_ * 8 + x_ * 2 + c_, blk)

    core_id = dp_id(z, x, 1 - core)
    x_ids = [dp_id(z, (x + d) % X, core) for d in (1, 2, 3)]
    z_ids = [dp_id((z + d) % Z, x, core) for d in (1, 2, 3)]
    everyone = [(dp, blk_peer(dy, dz)) for dy, dz in OFFS] + [core_id] + x_ids + z_ids

    barrier = pltpu.get_barrier_semaphore()
    for who in everyone:
        pl.semaphore_signal(barrier, inc=1, device_id=who, device_id_type=MESH)

    def remote(src, dst, ss, rs, who):
        copy = pltpu.make_async_remote_copy(
            src_ref=src, dst_ref=dst, send_sem=ss, recv_sem=rs, device_id=who, device_id_type=MESH
        )
        copy.start()
        pending.append(copy)
        return copy

    def exchange(name):
        s, d, ss, rs = (v[k + name] for k in ("s_", "r_", "ss_", "rs_"))
        out = {}
        for i, (dy, dz) in enumerate(OFFS):
            p = blk_peer(dy, dz)
            out[dy, dz] = remote(s.at[p], d.at[blk], ss.at[i], rs.at[i], (dp, p))
        d[blk] = s[blk]
        return out

    def pairs(name, copies, matrix, use):
        for dy in range(4):
            for dz in range(2):
                if (dy, dz) != (0, 0):
                    copies[dy, dz].wait_recv()
            ys = (y - dy + Y) % Y
            two = v["r_" + name][pl.ds(ys * 2, 2)].reshape(224, 2 * T)
            use(ys, nn(matrix[...], two))

    def unswap(source, wide, out):
        def one(s):
            got = source(s).astype(F32).reshape(4, 4, 8, T)
            for a in range(4):
                for b in range(4):
                    wide[b, s, a] = got[a, b]

        loop(8, one)
        for b in range(KB):
            out[b] = wide[b].reshape(DB, T).astype(BF)

    def arrived(copies):
        for copy in copies.values():
            copy.wait_recv()

    def sent(copies):
        for copy in copies.values():
            copy.wait_send()
        gone = {id(copy) for copy in copies.values()}
        pending[:] = [copy for copy in pending if id(copy) not in gone]

    need(*INPUTS[:FIRST])
    load(*INPUTS[FIRST:])
    for k in range(KB):
        xk = r.v_x[:, k * DB : (k + 1) * DB]
        r.flow[k, :, :T] = nt(r.v_wgr[k], xk)
        r.flow[k, :, T:] = nt(r.v_wur[k], xk)
    for p in range(8):
        rows = r.flow[:, p * 56 : (p + 1) * 56, :].reshape(224, 2 * T).astype(BF)
        taken = nn(r.v_take[...], rows).astype(BF)
        r.s_a0[p] = taken[:112]
        r.s_a1[p] = taken[112:]
    pl.semaphore_wait(barrier, len(everyone))
    from_a = [exchange("a0")]

    need("wdl", "g")
    r.dl[...] = jnp.swapaxes(r.v_wdl[...], 0, 1)
    for j in range(KB):
        f = nt(r.dl[j], r.v_g[:, j * DB : (j + 1) * DB]).astype(BF)
        r.s_c[:, j * 32 : (j + 1) * 32, :] = f.reshape(8, 32, T)

    need("wgl", "wul", "wdr", "meet", "order", "turn", "back", "spread", "twin")
    r.gl[...] = jnp.swapaxes(r.v_wgl[...], 0, 1)
    r.ul[...] = jnp.swapaxes(r.v_wul[...], 0, 1)
    eye = lax.broadcasted_iota(jnp.int32, (DB, DB), 0) == lax.broadcasted_iota(jnp.int32, (DB, DB), 1)
    eye = eye.astype(F32).astype(BF)
    swapped = jnp.swapaxes(r.v_wdr[...], 0, 1)
    for k in range(KB):
        r.dr[k] = nt(eye, swapped[k]).astype(BF)
    r.rhs_gright[...] = jnp.zeros_like(r.rhs_gright)
    r.rhs_uright[...] = jnp.zeros_like(r.rhs_uright)
    for k in range(KB):
        f = nt(r.v_order[...], r.v_x[:, k * DB : (k + 1) * DB]).astype(BF)
        r.lhs_right[:, :, k * T : (k + 1) * T] = f.reshape(2, 128, T)

    def turned(k):
        r.turned_g[k] = nn(r.v_turn[...], r.v_wgr[k]).astype(BF).reshape(2, 224, DB)
        r.turned_u[k] = nn(r.v_turn[...], r.v_wur[k]).astype(BF).reshape(2, 224, DB)

    loop(KB, turned)

    def forward(h):
        def keep(ys, moved):
            r.seen[2 * h : 2 * h + 2, pl.ds(ys, 1)] = moved.astype(BF).reshape(2, 1, 112, 2 * T)

        pairs("a%d" % h, from_a[h], r.v_meet, keep)
        for i in range(2):
            j = 2 * h + i
            seen = r.seen[j].reshape(MB, 2 * T)
            pre = tn(seen[:, :T], r.gl[j])
            up = tn(seen[:, T:], r.ul[j])
            sig = jax.nn.sigmoid(pre)
            act = pre * sig
            hidden = (act * up).astype(BF)
            r.act[j] = act
            r.slope[j] = up * sig * (1.0 + pre * (1.0 - sig))
            r.hidden[j] = hidden
            f = nt(r.dr[j], hidden).astype(BF)
            v["s_b%d" % h][:, i * 32 : (i + 1) * 32, :] = f.reshape(8, 32, T)

    def backward(h):
        for i in range(2):
            j = 2 * h + i
            hf = tn(r.dback[j], r.dr[j])
            gg = (hf * r.slope[j]).astype(BF)
            ug = (hf * r.act[j]).astype(BF)
            r.flow[i, :, :T] = nt(r.gl[j], gg)
            r.flow[i, :, T:] = nt(r.ul[j], ug)
            r.rhs_left[j, :T, :] = jnp.concatenate([gg, jnp.zeros((T, MB), BF)], axis=1)
            r.rhs_left[j, T:, :] = jnp.concatenate([jnp.zeros((T, MB), BF), ug], axis=1)
        for p in range(8):
            rows = r.flow[:2, p * 56 : (p + 1) * 56, :].reshape(112, 2 * T)
            v["s_d%d" % h][p] = rows.astype(BF)

    moves = {}

    def start_core(name, which, half):
        s0, r0, ss, rs = (v[k + name] for k in ("s0_", "r0_", "ss0_", "rs0_"))
        for j in which:
            s0[j] = half(j, 1 - core).astype(BF)
            moves[name, 0, j] = remote(s0.at[j], r0.at[j], ss.at[j], rs.at[j], core_id)

    def start_x(name, which, half):
        r0, s1, r1, ss, rs = (v[k + name] for k in ("r0_", "s1_", "r1_", "ss1_", "rs1_"))
        for j in which:
            own = half(j, core)
            moves[name, 0, j].wait_recv()
            s1[j] = (own + r0[j].astype(F32)).astype(BF).reshape(s1.shape[1:])
            for i in (0, 2, 1):
                moves[name, 1, j, i] = remote(
                    s1.at[j, (x + i + 1) % X],
                    r1.at[j, i],
                    ss.at[j * 3 + i],
                    rs.at[j * 3 + i],
                    x_ids[i],
                )

    def start_z(name, count):
        s1, r1, s2, r2, ss, rs = (
            v[k + name] for k in ("s1_", "r1_", "s2_", "r2_", "ss2_", "rs2_")
        )
        for j in range(count):
            for i in range(3):
                moves[name, 1, j, i].wait_recv()
            total = s1[j, x].astype(F32)
            for i in range(3):
                total = total + r1[j, i].astype(F32)
            s2[j] = total.astype(BF).reshape(s2.shape[1:])
        for i in range(3):
            moves[name, 2, i] = remote(
                s2.at[:, (z + i + 1) % Z], r2.at[i], ss.at[i], rs.at[i], z_ids[i]
            )

    def start_pair(name, count):
        s1, r1, s2, r2, ss, rs = (
            v[k + name] for k in ("s1_", "r1_", "s2_", "r2_", "ss2_", "rs2_")
        )
        for j in range(count):
            for i in range(3):
                moves[name, 1, j, i].wait_recv()
            total = s1[j, x].astype(F32)
            for i in range(3):
                total = total + r1[j, i].astype(F32)
            s2[j] = total.astype(BF).reshape(s2.shape[1:])
        near = z + 1 - 2 * (z % 2)
        moves[name, 2] = remote(
            s2.at[:, :, 1 - z % 2], r2, ss.at[0], rs.at[0], dp_id(near, x, core)
        )

    def start_far(name, count):
        s2, r2, s3, r3, ss, rs = (
            v[k + name] for k in ("s2_", "r2_", "s3_", "r3_", "ss2_", "rs2_")
        )
        moves[name, 2].wait_recv()
        for j in range(count):
            for i in range(2):
                s3[j, i] = (s2[j, i, z % 2].astype(F32) + r2[j, i].astype(F32)).astype(BF)
        moves[name, 3] = remote(
            s3.at[:, 1 - z // 2], r3, ss.at[1], rs.at[1], dp_id((z + 2) % Z, x, core)
        )

    def finish_far(name, count):
        s3, r3, out = v["s3_" + name], v["r3_" + name], v["o_" + name]
        moves[name, 3].wait_recv()
        for j in range(count):
            out[j] = scale * (s3[j, z // 2].astype(F32) + r3[j].astype(F32))

    def finish(name, count):
        s2, r2, out = v["s2_" + name], v["r2_" + name], v["o_" + name]
        for i in range(3):
            moves[name, 2, i].wait_recv()
        for j in range(count):
            total = s2[j, z].astype(F32)
            for i in range(3):
                total = total + r2[i, j].astype(F32)
            out[j] = scale * total

    def sides(h):
        for j in (2 * h, 2 * h + 1):
            f = nn(r.v_spread[...], r.seen[j].reshape(MB, 2 * T)).astype(BF)
            r.lhs_left[j] = f.reshape(2, 256, 2 * T)
            f = nt(r.v_spread[...], r.hidden[j]).astype(BF)
            r.lhs_dright[j] = f.reshape(2, 256, T)

    def dleft_half(q, c):
        rows = [r.v_g[:, (2 * q + i) * DB : (2 * q + i + 1) * DB] for i in range(2)]
        return nn(r.lhs_dleft[q, c], jnp.concatenate(rows, axis=0))

    def right_half(j, c):
        both = [nt(r.lhs_right[c], rhs[...]) for rhs in (r.rhs_gright, r.rhs_uright)]
        both = [part.reshape(16, 1, 8, 896) for part in both]
        return jnp.concatenate(both, axis=1).reshape(256, 896)

    def token_part(h, k):
        part = tn(r.back[k, :, :T], r.turned_g[k, h])
        return part + tn(r.back[k, :, T:], r.turned_u[k, h])

    def right(h):
        def keep(ys, moved):
            r.back32[:, pl.ds(ys, 1)] = moved.reshape(KB, 1, 56, 2 * T)

        pairs("d%d" % h, from_d[h], r.v_back, keep)
        for k in range(KB):
            back = r.back32[k].reshape(224, 2 * T).astype(BF)
            r.back[k] = back
            r.rhs_gright[k * 224 : (k + 1) * 224, k * T : (k + 1) * T] = back[:, :T]
            r.rhs_uright[k * 224 : (k + 1) * 224, k * T : (k + 1) * T] = back[:, T:]
        start_core("right%d" % h, (0,), right_half)

    def left(h):
        sides(h)
        parts = [
            ("left%d" % h, (0, 1), lambda i, c: nn(r.lhs_left[2 * h + i, c], r.rhs_left[2 * h + i])),
            ("dright%d" % h, (0, 1), lambda i, c: nt(r.lhs_dright[2 * h + i, c], r.dback[2 * h + i])),
        ]
        for part in parts:
            start_core(*part)
        for part in parts:
            start_x(*part)

    sent(from_a[0])
    from_c = exchange("c")
    forward(0)
    sent(from_c)
    from_a.append(exchange("a1"))
    arrived(from_c)
    unswap(lambda s: r.r_c[s], r.dback32, r.dback)
    backward(0)
    left(0)
    sent(from_a[1])
    from_d = [exchange("d0")]
    forward(1)
    backward(1)
    left(1)
    sent(from_d[0])
    from_d.append(exchange("d1"))

    right(0)
    for k in range(KB):
        r.tok[:, k * DB : (k + 1) * DB] = token_part(0, k)
    start_x("right0", (0,), right_half)
    from_b = [exchange("b0"), exchange("b1")]

    for name in ("left0", "dright0", "left1", "dright1"):
        start_pair(name, 2)

    right(1)
    start_far("left0", 2)
    start_far("dright0", 2)
    start_x("right1", (0,), right_half)
    start_far("left1", 2)
    start_far("dright1", 2)
    start_z("right0", 1)

    for copies in from_b:
        arrived(copies)
    unswap(lambda s: jnp.concatenate([r.r_b0[s], r.r_b1[s]], axis=0), r.dseen32, r.dseen)
    for j in range(KB):
        f = nn(r.v_twin[j % 2], r.dseen[j]).astype(BF)
        r.lhs_dleft[j // 2, :, :, (j % 2) * T : (j % 2 + 1) * T] = f.reshape(2, 256, T)
    start_core("dleft", (0, 1), dleft_half)
    for k in range(KB):
        columns = slice(k * DB, (k + 1) * DB)
        r.w_gtok[:, columns] = (r.tok[:, columns] + token_part(1, k)).astype(BF)
    out_gtok = pltpu.make_async_copy(r.w_gtok, r.gtok, r.out_sem.at[0])
    out_gtok.start()
    start_x("dleft", (0, 1), dleft_half)
    start_z("right1", 1)
    start_z("dleft", 2)
    for j in range(KB):
        r.w_mixed[:, j * DB : (j + 1) * DB] = tn(r.dseen[j], r.dl[j]).astype(BF)
    out_mixed = pltpu.make_async_copy(r.w_mixed, r.mixed, r.out_sem.at[1])
    out_mixed.start()
    finish("right0", 1)
    for name in PAIRED:
        finish_far(name, 2)
    finish("right1", 1)
    finish("dleft", 2)
    out_gtok.wait()
    out_mixed.wait()
    for copy in pending:
        copy.wait_send()


def unpack(names, *refs):
    r = types.SimpleNamespace(**dict(zip(names, refs)))
    copies = [
        pltpu.make_async_copy(r.mixed_in, r.mixed_held, r.sem.at[0]),
        pltpu.make_async_copy(r.gtok_in, r.gtok_held, r.sem.at[1]),
    ]
    for i, name in enumerate(UNPACKED):
        copies.append(pltpu.make_async_copy(vars(r)["h_" + name], vars(r)[name], r.sem.at[2 + i]))
    for copy in copies:
        copy.start()
    for copy in copies:
        copy.wait()
    onward = [
        pltpu.make_async_copy(r.mixed_held, r.mixed, r.out_sem.at[0]),
        pltpu.make_async_copy(r.gtok_held, r.gtok, r.out_sem.at[1]),
    ]
    for copy in onward:
        copy.start()
    total = None
    for h, source in enumerate((r.right0, r.right1)):
        rows = source[0]
        parts = [rows[:, :256]] + [pltpu.roll(rows, 896 - 224 * k, 1)[:, :256] for k in (1, 2, 3)]
        part = lax.dot_general(
            jnp.concatenate(parts, axis=0),
            r.columns[h],
            (((1,), (0,)), ((), ())),
            precision=lax.Precision.HIGHEST,
            preferred_element_type=F32,
        )
        total = part if total is None else total + part
    for k in range(KB):
        r.gr[:, k, :] = total[k * 16 : k * 16 + 8]
        r.ur[:, k, :] = total[k * 16 + 8 : k * 16 + 16]
    for j in range(KB):
        rows = (r.left0, r.left1)[j // 2][j % 2]
        r.gl[:, j, :] = rows[:MS, :MB]
        r.ul[:, j, :] = rows[:MS, MB:]
        r.dr[:, j, :] = (r.dright0, r.dright1)[j // 2][j % 2][:MS]
        r.dl[:, j, :] = r.dleft[j // 2][(j % 2) * 8 : (j % 2 + 1) * 8]
    for copy in onward:
        copy.wait()


def local(tokens, gate_right, gate_left, upward_right, upward_left, down_right, down_left, cotangent):
    scale = float(tokens.shape[0] * lax.axis_size("dp")) ** (-0.5)
    given = {
        "x": tokens,
        "g": cotangent,
        "wgr": jnp.transpose(gate_right, (1, 2, 0)),
        "wur": jnp.transpose(upward_right, (1, 2, 0)),
        "wdl": down_left,
        "wgl": gate_left,
        "wul": upward_left,
        "wdr": down_right,
    }
    given.update({name: jnp.asarray(value) for name, value in permutations().items()})
    scratch = scratch_list()
    names = ["h_" + name for name in INPUTS] + list(OUTS) + [name for name, _ in scratch]
    shapes = [jax.ShapeDtypeStruct((T, KB * DB), BF)] * 2
    shapes += [jax.ShapeDtypeStruct((count, 16, lanes), F32) for _, count, lanes in GROUPS]

    def body(*refs):
        kernel(scale, names, *refs)

    results = pl.pallas_call(
        body,
        out_shape=shapes,
        in_specs=[pl.BlockSpec(memory_space=pl.ANY)] * len(INPUTS),
        out_specs=[pl.BlockSpec(memory_space=pl.ANY)] * 2
        + [pl.BlockSpec(memory_space=pltpu.VMEM)] * (len(OUTS) - 2),
        scratch_shapes=[shape for _, shape in scratch],
        compiler_params=pltpu.CompilerParams(
            collective_id=0, has_side_effects=True, vmem_limit_bytes=VMEM_LIMIT
        ),
        name="monarch",
    )(*[given[name] for name in INPUTS])

    last = [
        ((T, KB * DB), BF),
        ((T, KB * DB), BF),
        ((8, KB, MB), F32),
        ((MS, KB, MB), F32),
        ((8, KB, MB), F32),
        ((MS, KB, MB), F32),
        ((MS, KB, DB), F32),
        ((8, KB, DB), F32),
    ]
    anywhere, vmem = pl.BlockSpec(memory_space=pl.ANY), pl.BlockSpec(memory_space=pltpu.VMEM)
    parts = list(results[2:]) + [jnp.asarray(untangle())]
    names = ["mixed_in", "gtok_in"] + ["h_" + name for name in UNPACKED]
    names += ["mixed", "gtok", "gr", "gl", "ur", "ul", "dr", "dl"] + list(UNPACKED)
    names += ["mixed_held", "gtok_held", "sem", "out_sem"]
    return pl.pallas_call(
        lambda *refs: unpack(names, *refs),
        out_shape=[jax.ShapeDtypeStruct(*entry) for entry in last],
        in_specs=[anywhere] * (2 + len(parts)),
        out_specs=[anywhere] * 2 + [vmem] * 6,
        scratch_shapes=[pltpu.VMEM(part.shape, F32) for part in parts]
        + [pltpu.VMEM((T, KB * DB), BF)] * 2
        + [pltpu.SemaphoreType.DMA((2 + len(parts),)), pltpu.SemaphoreType.DMA((2,))],
        compiler_params=pltpu.CompilerParams(vmem_limit_bytes=VMEM_LIMIT),
        name="unpack",
    )(*results[:2], *parts)


def solution(mesh):
    weight = P(None, "blk", None)
    grad = P("dp", "blk", None)
    return jax.shard_map(
        local,
        mesh=mesh,
        in_specs=(P("dp", "blk"),) + (weight,) * 6 + (P("dp", "blk"),),
        out_specs=(P("dp", "blk"),) * 2 + (grad,) * 6,
        check_vma=False,
    )
```
